256 devices in a mesh: pipe: 4 (over x), dp: 16 (over z, core), mp: 4 (over y).
Axes of the slice: x: 4, y: 4, z: 8, core: 2. Of those that a mesh axis runs over, the one named last changes fastest.
Arguments:
- queries: bfloat16 [4, 4, 2048, 8192], P('pipe', None, 'dp', 'mp'), may hold values from -6 to 6
- grad_out: bfloat16 [4, 4, 2048, 8192], P('pipe', None, 'dp', 'mp'), may hold values from -6 to 6
- features: bfloat16 [4, 2048, 8192], P('pipe', 'dp', 'mp'), may hold values from -6 to 6
- w_key: bfloat16 [4, 8192, 1024], P('pipe', ('mp', 'dp')), may hold values from -0.0625 to 0.0625
- w_value: bfloat16 [4, 8192, 1024], P('pipe', ('mp', 'dp')), may hold values from -0.0625 to 0.0625
- q_gain: float32 [4, 128], P('pipe'), may hold values from 0.1 to 1.9
- k_gain: float32 [4, 128], P('pipe'), may hold values from 0.1 to 1.9
- tile_counts: int32 [4, 16, 2], P(None, 'dp'), may hold values from 1 to 4, as said below
- image_starts: int32 [4, 16, 2], P(None, 'dp'), may hold values from 0 to 127, as said below
Outputs:
- feature_grads: bfloat16 [4, 2048, 8192], P('pipe', 'dp', 'mp')
- key_weight_grads: bfloat16 [4, 8192, 1024], P('pipe', ('mp', 'dp'))
- value_weight_grads: bfloat16 [4, 8192, 1024], P('pipe', ('mp', 'dp'))
The draws below stay inside these ranges and needn't reach their ends.
Inputs may be any that keep to these rules, and one draw needn't show every extreme that they name: `tile_counts`: every image has at least one tile, and some image of some bin has 4 tiles. `image_starts`: within a bin the images' positions never fall.
All inputs are finite; a program needn't handle non-finite values.
Results may differ from the reference program's by a relative error of at most 0.028.
Values may be sent and summed in bfloat16 or wider, within the bound.
A program may use at most 128 MiB of HBM per device.

```python
import math
import jax
import jax.numpy as jnp
from jax import lax

D = 8192
HD = 128
TOK = 128
TILE_TOK = 16
NIMG = 2
MAX_TILES = 4
M = 4
SECTIONS = 4
QW = 8192
KVW = 1024
TOKENS = 2048
IMAGES = 2048
N_DP = 16


def draw_tile_counts(key, part):
    values = jax.random.randint(key, (M, N_DP, NIMG), 1, MAX_TILES + 1, dtype=jnp.int32)
    return values.at[0, 0, 0].set(MAX_TILES)


def draw_image_starts(key, part):
    lead_key = jax.random.fold_in(key, 11)
    step_key = jax.random.fold_in(key, 23)
    leading = jax.random.randint(lead_key, (M, N_DP, 1), 0, TOK // 2, dtype=jnp.int32)
    increments = jax.random.randint(step_key, (M, N_DP, NIMG - 1), 0, TOK // 2, dtype=jnp.int32)
    return jnp.concatenate([leading, leading + jnp.cumsum(increments, axis=-1)], axis=-1)


def with_spikes(values, key, source, target, parts, factor):
    def block_of(axis_at):
        return (jnp.arange(values.shape[axis_at]) // (values.shape[axis_at] // parts)).reshape((-1,) + (1,) * (values.ndim - 1 - axis_at))

    near = jax.random.permutation(key, parts)[block_of(target)]
    second = (block_of(target) + parts // 2) % parts
    return jnp.where((block_of(source) == near) | (block_of(source) == second), factor * values, values)


def block_scale(own_key, dims, shards, low, top_value):
    def one(position, parts):
        steps = jax.random.uniform(jax.random.fold_in(jax.random.fold_in(own_key, 6), position), (parts,), jnp.float32, low / len(shards), top_value / len(shards))
        return jnp.repeat(jnp.exp(steps), dims[position] // parts).reshape((-1,) + (1,) * (len(dims) - position - 1))

    level = one(*shards[0])
    for cut in shards[1:]:
        level = level * one(*cut)
    return level


def centred(own_key, shape, width, limit, cuts=(), held_as=jnp.bfloat16):
    level = block_scale(own_key, shape, cuts, -0.22, 0.18) if cuts else 1.0
    values = jax.random.normal(own_key, shape, jnp.float32) * width * level
    return jnp.minimum(jnp.maximum(values, -limit), limit).astype(held_as)


def heavy_noise(own_key, shape, scale, limit, pieces, heavy, kind=jnp.bfloat16):
    result = scale * jax.random.normal(own_key, shape, jnp.float32)
    if pieces:
        result = result * block_scale(own_key, shape, pieces, -0.22, 0.18)
    return jnp.clip(with_spikes(result, jax.random.fold_in(own_key, 3), *heavy), -limit, limit).astype(kind)


def setup_inputs(seed: int = 0) -> dict:
    splits = jax.random.split(jax.random.key(seed), 10)
    queries = centred(splits[0], (SECTIONS, M, TOKENS, QW), 1.0, 6.0, ((0, 4), (2, 16), (3, 4)))
    grad_out = centred(splits[1], (SECTIONS, M, TOKENS, QW), 1.0, 6.0, ((0, 4), (2, 16), (3, 4)))
    features = heavy_noise(splits[2], (M, IMAGES, D), 1.0, 6.0, ((0, 4), (1, 16), (2, 4)), (1, 2, 16, 2.0))
    w_key = centred(splits[3], (SECTIONS, D, KVW), D ** -0.5, 0.0625, ((0, 4), (1, 64)))
    w_value = centred(splits[4], (SECTIONS, D, KVW), D ** -0.5, 0.0625, ((0, 4), (1, 64)))
    q_gain = jnp.clip(1.0 + 0.18 * jax.random.normal(splits[5], (SECTIONS, HD), jnp.float32), 0.1, 1.9)
    k_gain = jnp.clip(1.0 + 0.18 * jax.random.normal(splits[6], (SECTIONS, HD), jnp.float32), 0.1, 1.9)
    tile_counts = draw_tile_counts(jax.random.fold_in(splits[9], 71), 0)
    image_starts = draw_image_starts(jax.random.fold_in(splits[9], 71), 0)
    return {"queries": queries, "grad_out": grad_out, "features": features, "w_key": w_key, "w_value": w_value, "q_gain": q_gain, "k_gain": k_gain, "tile_counts": tile_counts, "image_starts": image_starts}


EPSILON = 1e-05

def normed(values, gain):
    inverse = lax.rsqrt(lax.optimization_barrier(jnp.mean(values * values, axis=-1, keepdims=True)) + EPSILON)
    return values * inverse * gain

def visible_slots(tile_counts, image_starts, image_len, text_len):
    lengths = tile_counts * TILE_TOK
    image_upper = jnp.cumsum(lengths, axis=-1)
    image_lower = image_upper - lengths
    slot_index = jnp.arange(image_len, dtype=jnp.int32)
    text_index = jnp.arange(text_len, dtype=jnp.int32)
    inside = ((slot_index >= image_lower[..., None]) & (slot_index < image_upper[..., None])).astype(jnp.float32)
    text_after = (text_index >= image_starts[..., None]).astype(jnp.float32)
    return jnp.einsum('...ij,...it->...jt', inside, text_after)

def attention_grads(query, grad_out, key_pre, value_rounded, visible, q_gain, k_gain):
    root_scale = 1.0 / math.sqrt(query.shape[-1])
    query_normed = normed(query.astype(jnp.float32), q_gain).astype(jnp.bfloat16)
    key_normed = normed(key_pre, k_gain).astype(jnp.bfloat16)
    scores = jnp.einsum('bjgd,btghd->bghjt', key_normed.astype(jnp.float32), query_normed.astype(jnp.float32)) * root_scale
    weights = jnp.exp(scores) * visible[:, None, None]
    denominator = lax.optimization_barrier(jnp.sum(weights, axis=3, keepdims=True))
    probability = weights / jnp.where(denominator > 0, denominator, 1.0)
    prob_rounded = probability.astype(jnp.bfloat16)
    value_grad = jnp.einsum('bghjt,btghd->bjgd', prob_rounded.astype(jnp.float32), grad_out.astype(jnp.float32)).astype(jnp.bfloat16)
    prob_grad = jnp.einsum('btghd,bjgd->bghjt', grad_out.astype(jnp.float32), value_rounded.astype(jnp.float32))
    row_delta = lax.optimization_barrier(jnp.sum(probability * prob_grad, axis=3, keepdims=True))
    score_grad = (probability * (prob_grad - row_delta)).astype(jnp.bfloat16)
    normed_grad = jnp.einsum('bghjt,btghd->bjgd', score_grad.astype(jnp.float32), query_normed.astype(jnp.float32)) * root_scale
    inverse = lax.rsqrt(lax.optimization_barrier(jnp.mean(key_pre * key_pre, axis=-1, keepdims=True)) + EPSILON)
    scaled = normed_grad * k_gain
    key_grad = inverse * scaled - key_pre * inverse ** 3 * lax.optimization_barrier(jnp.mean(scaled * key_pre, axis=-1, keepdims=True))
    return (key_grad.astype(jnp.bfloat16), value_grad)

def reference(queries, grad_out, features, w_key, w_value, q_gain, k_gain, tile_counts, image_starts):
    micro_count, image_count, model_width = features.shape
    replica_count = tile_counts.shape[1]
    image_len = image_count // replica_count
    text_len = queries.shape[2] // replica_count
    key_width = w_key.shape[2]
    head_dim = q_gain.shape[1]
    key_heads = key_width // head_dim
    groups = queries.shape[3] // key_width
    visible = visible_slots(tile_counts, image_starts, image_len, text_len)
    shape_q = (replica_count, text_len, key_heads, groups, head_dim)
    shape_k = (replica_count, image_len, key_heads, head_dim)
    factor = 1.0 / (micro_count * replica_count)

    def one_section(image_total, inputs):
        query_section, grad_section, key_weight, value_weight, query_gain, key_gain = inputs

        def one_batch(batch):
            feature_bin, query_bin, grad_bin, visible_bin = batch
            key_pre = jnp.dot(feature_bin, key_weight, preferred_element_type=jnp.float32)
            value_rounded = jnp.dot(feature_bin, value_weight, preferred_element_type=jnp.float32).astype(jnp.bfloat16)
            key_grad, value_grad = attention_grads(query_bin.reshape(shape_q), grad_bin.reshape(shape_q), key_pre.reshape(shape_k), value_rounded.reshape(shape_k), visible_bin, query_gain, key_gain)
            key_grad = key_grad.reshape(image_count, key_width)
            value_grad = value_grad.reshape(image_count, key_width)
            projected = jnp.dot(key_grad, key_weight.T, preferred_element_type=jnp.float32) + jnp.dot(value_grad, value_weight.T, preferred_element_type=jnp.float32)
            return (key_grad, value_grad, projected)
        key_grads, value_grads, projected = lax.map(one_batch, (features, query_section, grad_section, visible))

        def replica_term(totals, replica):
            start = (replica * image_len).astype(jnp.int32)
            feature_rows = lax.dynamic_slice_in_dim(features, start, image_len, 1).reshape(micro_count * image_len, model_width)
            key_rows = lax.dynamic_slice_in_dim(key_grads, start, image_len, 1).reshape(micro_count * image_len, key_width)
            value_rows = lax.dynamic_slice_in_dim(value_grads, start, image_len, 1).reshape(micro_count * image_len, key_width)
            key_term = jnp.dot(feature_rows.T, key_rows, preferred_element_type=jnp.float32).astype(jnp.bfloat16)
            value_term = jnp.dot(feature_rows.T, value_rows, preferred_element_type=jnp.float32).astype(jnp.bfloat16)
            key_term, value_term = lax.optimization_barrier((key_term, value_term))
            return ((totals[0] + key_term.astype(jnp.float32), totals[1] + value_term.astype(jnp.float32)), None)
        zeros = jnp.zeros((model_width, key_width), jnp.float32)
        totals, unused = lax.scan(replica_term, (zeros, zeros), jnp.arange(replica_count, dtype=jnp.int32))
        key_out = (totals[0] * factor).astype(jnp.bfloat16)
        value_out = (totals[1] * factor).astype(jnp.bfloat16)
        return (image_total + projected, (key_out, value_out))
    image_total, outs_pair = lax.scan(one_section, jnp.zeros(features.shape, jnp.float32), (queries, grad_out, w_key, w_value, q_gain, k_gain))
    return (image_total.astype(jnp.bfloat16), outs_pair[0], outs_pair[1])
```

```python
import math

import jax
import jax.numpy as jnp
from jax import lax
from jax.experimental import pallas as pl
from jax.experimental.pallas import tpu as pltpu
from jax.sharding import PartitionSpec as P

TILE_TOK = 16
EPSILON = 1e-05
NX, NY, NZ = 4, 4, 8
HD = 128
ROWS = 128
WIDTH = 2048
GROUPS = 8
OFFSETS = (0, 1, 3, 2)
RIGHT, LEFT = 0, 1
HALF = NZ // 2
BF = jnp.bfloat16
F32 = jnp.float32
MESH = pl.DeviceIdType.MESH
N_SEMS = 224
NT = (((1,), (1,)), ((), ()))


def kernel(
    queries,
    grad_out,
    features,
    w_key,
    w_value,
    q_gain,
    k_gain,
    tiles,
    starts,
    out_f,
    out_k,
    out_v,
    qb,
    do,
    fa,
    ft,
    wb,
    ps,
    rk,
    gs,
    ga,
    pw,
    sb,
    rb,
    osd,
    ow,
    ds,
    dr,
    dk,
    dx,
    xr,
    send_sems,
    recv_sems,
    local_sems,
):
    px = lax.axis_index("pipe")
    dd = lax.axis_index("dp")
    qy = lax.axis_index("mp")
    zz = dd // 2
    cc = dd % 2
    oc = 1 - cc
    kinds = (w_key, w_value)

    def at_x(step):
        return ((px + step) % NX, dd, qy)

    def at_y(step, core):
        return (px, zz * 2 + core, (qy + step) % NY)

    def at_z(step):
        return (px, ((zz + step) % NZ) * 2 + cc, qy)

    sibling = (px, zz * 2 + oc, qy)

    ids = {}
    started = []

    def sem_of(key):
        return ids.setdefault(key, len(ids))

    def remote(key, src, dst, device):
        n = sem_of(key)
        return pltpu.make_async_remote_copy(
            src_ref=src,
            dst_ref=dst,
            send_sem=send_sems.at[n],
            recv_sem=recv_sems.at[n],
            device_id=device,
            device_id_type=MESH,
        )

    def send(key, src, dst, device):
        copy = remote(key, src, dst, device)
        copy.start()
        started.append(copy)

    def receive(key, dst):
        remote(key, dst, dst, sibling).wait_recv()

    local_ids = {}

    def local(key, src, dst):
        n = local_ids.setdefault(key, len(local_ids))
        return pltpu.make_async_copy(src, dst, local_sems.at[n])

    barrier = pltpu.get_barrier_semaphore()
    partners = [sibling, at_z(1), at_z(NZ - 1)]
    partners += [at_x(step) for step in (1, 2, 3)]
    partners += [at_y(step, core) for step in (1, 2, 3) for core in (cc, oc)]
    for device in partners:
        pl.semaphore_signal(barrier, inc=1, device_id=device, device_id_type=MESH)

    def weight_columns(ref, hh, j):
        return ref.at[0, :, pl.ds((2 * j + hh) * HD, HD)]

    for kind in (0, 1):

        @pl.when(cc == kind)
        def _():
            for hh in (0, 1):
                for j in range(NY):
                    local(
                        ("w", hh, j),
                        weight_columns(kinds[kind], hh, j),
                        wb.at[hh, zz, cc, :, pl.ds(j * HD, HD)],
                    ).start()

    local("f", features.at[0], fa.at[0, cc]).start()
    for slot in range(NX):
        local(("q", slot), queries.at[0, (px + OFFSETS[slot]) % NX], qb.at[slot]).start()
        local(("d", slot), grad_out.at[0, (px + OFFSETS[slot]) % NX], do.at[slot]).start()

    pl.semaphore_wait(barrier, len(partners))

    for kind in (0, 1):

        @pl.when(oc == kind)
        def _():
            for hh in (0, 1):
                for j in range(NY):
                    remote(
                        ("w", hh, j),
                        weight_columns(kinds[kind], hh, j),
                        wb.at[hh, zz, cc, :, pl.ds(j * HD, HD)],
                        sibling,
                    ).start()

    for hh in (0, 1):
        for j in range(NY):
            piece = wb.at[hh, zz, cc, :, pl.ds(j * HD, HD)]
            started.append(remote(("w", hh, j), piece, piece, sibling))

    send(("fx", 3), features.at[0], fa.at[2, cc], at_x(1))
    send(("fx", 1), features.at[0], fa.at[1, cc], at_x(3))
    send(("fs", 0), features.at[0], fa.at[0, cc], sibling)

    def gather_pieces(direction, k):
        if k == HALF - 1:
            return (direction,)
        return (0, 1)

    def origin(direction, k):
        return (zz - k + NZ) % NZ if direction == RIGHT else (zz + k) % NZ

    def gather_send(hh, k, pieces=(0, 1)):
        for piece in pieces:
            for direction in (RIGHT, LEFT):
                if piece not in gather_pieces(direction, k):
                    continue
                block = wb.at[hh, origin(direction, k), piece]
                if k:
                    receive(("ag", direction, hh, k - 1, piece), block)
                send(
                    ("ag", direction, hh, k, piece),
                    block,
                    block,
                    at_z(1 if direction == RIGHT else NZ - 1),
                )

    def gather_rest(hh):
        for direction in (RIGHT, LEFT):
            piece = 1 - direction
            receive(
                ("ag", direction, hh, HALF - 2, piece),
                wb.at[hh, origin(direction, HALF - 1), piece],
            )

    def gather_last(hh):
        for direction in (RIGHT, LEFT):
            receive(
                ("ag", direction, hh, HALF - 1, direction),
                wb.at[hh, origin(direction, HALF), direction],
            )

    def own_weights(hh):
        for j in range(NY):
            piece = wb.at[hh, zz, cc, :, pl.ds(j * HD, HD)]
            local(("w", hh, j), piece, piece).wait()
        for j in range(NY):
            piece = wb.at[hh, zz, oc, :, pl.ds(j * HD, HD)]
            receive(("w", hh, j), piece)

    def norm_queries(slot):
        local(("q", slot), qb.at[slot], qb.at[slot]).wait()
        gain = q_gain[...]

        def body(i, carry):
            for u in range(4):
                columns = pl.ds(pl.multiple_of((i * 4 + u) * HD, HD), HD)
                values = qb[slot, :, columns].astype(F32)
                inverse = lax.rsqrt(
                    jnp.mean(values * values, axis=-1, keepdims=True) + EPSILON
                )
                qb[slot, :, columns] = (values * inverse * gain).astype(BF)
            return carry

        lax.fori_loop(0, WIDTH // HD // 4, body, 0)

    def transpose_features(slot, replica):
        place = pl.multiple_of((slot * 2 + replica) * ROWS, ROWS)

        def body(i, carry):
            for u in range(2):
                columns = pl.ds(pl.multiple_of((i * 2 + u) * HD, HD), HD)
                ft[columns, pl.ds(place, ROWS)] = fa[slot, replica, :, columns].T
            return carry

        lax.fori_loop(0, WIDTH // HD // 2, body, 0)

    def project(hh, mg):
        def body(n, carry):
            rows = fa[2 * mg : 2 * mg + 2].reshape(4 * ROWS, WIDTH)
            columns = pl.ds(pl.multiple_of(n * 256, 256), 256)
            weights = wb[hh, :, :, :, columns].reshape(WIDTH, 256)
            total = jnp.dot(rows, weights, preferred_element_type=F32).astype(BF)
            for slot in (0, 1):
                for replica in (0, 1):
                    low = (slot * 2 + replica) * ROWS
                    for j in (0, 1):
                        ps[hh, replica, n * 2 + j, 2 * mg + slot] = total[
                            low : low + ROWS, j * HD : (j + 1) * HD
                        ]
            return carry

        lax.fori_loop(0, 2, body, 0)
        pair = pl.ds(2 * mg, 2)
        for step in (2, 1, 3, 0):
            target = (qy + step) % NY
            for same in (1, 0):
                core = cc if same else oc
                src = ps.at[hh, core, target, pair]
                dst = rk.at[hh, cc, step, pair]
                if step == 0 and same:
                    local(("kv", hh, mg), src, dst).start()
                else:
                    send(("kv", hh, mg, step, same), src, dst, at_y(step, core))

    def projected(hh, mg):
        pair = pl.ds(2 * mg, 2)
        for step in range(NY):
            for same in (1, 0):
                dst = rk.at[hh, cc if same else oc, step, pair]
                if step == 0 and same:
                    local(("kv", hh, mg), dst, dst).wait()
                else:
                    receive(("kv", hh, mg, step, same), dst)

    root_scale = 1.0 / math.sqrt(HD)

    def attend(hh, mg):
        gain = k_gain[...]

        def body(i, carry):
            slot = 2 * mg + i
            micro = (px + i) % NX if mg == 0 else (px + 3 - i) % NX
            key_pre = rk[hh, 0, 0, slot].astype(F32)
            value = rk[hh, 1, 0, slot].astype(F32)
            for step in range(1, NY):
                key_pre += rk[hh, 0, step, slot].astype(F32)
                value += rk[hh, 1, step, slot].astype(F32)
            value = value.astype(BF)
            inverse = lax.rsqrt(
                jnp.mean(key_pre * key_pre, axis=-1, keepdims=True) + EPSILON
            )
            key = (key_pre * inverse * gain).astype(BF)
            slots = lax.broadcasted_iota(jnp.int32, (ROWS, 2 * ROWS), 0)
            texts = lax.broadcasted_iota(jnp.int32, (ROWS, 2 * ROWS), 1) % ROWS
            first = tiles[micro, 0, 0] * TILE_TOK
            second = first + tiles[micro, 0, 1] * TILE_TOK
            seen = ((slots < first) & (texts >= starts[micro, 0, 0])) | (
                (slots >= first) & (slots < second) & (texts >= starts[micro, 0, 1])
            )
            visible = jnp.where(seen, 1.0, 0.0).astype(F32)
            value_grad = jnp.zeros((ROWS, HD), F32)
            normed_grad = jnp.zeros((ROWS, HD), F32)
            for g in range(0, GROUPS, 2):
                low = (hh * GROUPS + g) * HD
                query = jnp.concatenate(
                    [qb[slot, :, low : low + HD], qb[slot, :, low + HD : low + 2 * HD]], axis=0
                )
                grad = jnp.concatenate(
                    [do[slot, :, low : low + HD], do[slot, :, low + HD : low + 2 * HD]], axis=0
                )
                scores = (
                    lax.dot_general(key, query, NT, preferred_element_type=F32) * root_scale
                )
                weights = jnp.exp(scores) * visible
                total = jnp.sum(weights, axis=0, keepdims=True)
                probability = weights * (1.0 / jnp.where(total > 0, total, 1.0))
                prob_grad = lax.dot_general(value, grad, NT, preferred_element_type=F32)
                delta = jnp.sum(probability * prob_grad, axis=0, keepdims=True)
                score_grad = (probability * (prob_grad - delta)).astype(BF)
                value_grad += jnp.dot(
                    probability.astype(BF), grad, preferred_element_type=F32
                )
                normed_grad += jnp.dot(score_grad, query, preferred_element_type=F32)
            scaled = normed_grad * root_scale * gain
            key_grad = inverse * scaled - key_pre * (inverse * inverse * inverse) * jnp.mean(
                scaled * key_pre, axis=-1, keepdims=True
            )
            gs[hh, 0, slot] = key_grad.astype(BF)
            gs[hh, 1, slot] = value_grad.astype(BF)
            return carry

        lax.fori_loop(0, 2, body, 0)
        pair = pl.ds(2 * mg, 2)
        for step in (2, 1, 3, 0):
            for same in (1, 0):
                kind = cc if same else oc
                src = gs.at[hh, kind, pair]
                dst = ga.at[hh, qy, pair, cc]
                if step == 0 and same:
                    local(("g", hh, mg), src, dst).start()
                else:
                    send(("g", hh, mg, step, same), src, dst, at_y(step, kind))

    def gathered(hh, mg):
        pair = pl.ds(2 * mg, 2)
        for step in range(NY):
            source = (qy - step + NY) % NY
            for same in (1, 0):
                dst = ga.at[hh, source, pair, cc if same else oc]
                if step == 0 and same:
                    local(("g", hh, mg), dst, dst).wait()
                else:
                    receive(("g", hh, mg, step, same), dst)

    def weight_term(hh, distance):
        block = (zz + distance) % NZ
        lhs = ft[pl.ds(pl.multiple_of(block * 256, 256), 256), :]

        def body(n, carry):
            columns = pl.ds(pl.multiple_of(n * 256, 256), 256)
            grads = jnp.concatenate(
                [ga[hh, n * 2 + j].reshape(8 * ROWS, HD) for j in (0, 1)], axis=1
            )
            pw[distance, :, columns] = jnp.dot(lhs, grads, preferred_element_type=F32)
            return carry

        lax.fori_loop(0, 2, body, 0)

    def scatter_pieces(direction, k):
        return (direction,) if k == 0 else (0, 1)

    def scatter_send(hh, k, pieces=(0, 1)):
        for piece in pieces:
            for direction in (RIGHT, LEFT):
                if piece not in scatter_pieces(direction, k):
                    continue
                distance = HALF - k if direction == RIGHT else HALF + k
                total = pw[distance, piece * ROWS : (piece + 1) * ROWS, :]
                if k and piece in scatter_pieces(direction, k - 1):
                    arrived = rb.at[hh, direction, k - 1, piece]
                    receive(("rs", direction, hh, k - 1, piece), arrived)
                    total = total + arrived[...].astype(F32)
                sb[hh, direction, k, piece] = total.astype(BF)
                send(
                    ("rs", direction, hh, k, piece),
                    sb.at[hh, direction, k, piece],
                    rb.at[hh, direction, k, piece],
                    at_z(1 if direction == RIGHT else NZ - 1),
                )

    factor = 1.0 / (NX * NZ * 2)

    def scatter_last(hh):
        for direction in (RIGHT, LEFT):
            for piece in (0, 1):
                receive(
                    ("rs", direction, hh, HALF - 1, piece), rb.at[hh, direction, HALF - 1, piece]
                )

        def finished(piece):
            total = (
                pw[0, pl.ds(pl.multiple_of(piece * ROWS, ROWS), ROWS), :]
                + rb[hh, RIGHT, HALF - 1, piece].astype(F32)
                + rb[hh, LEFT, HALF - 1, piece].astype(F32)
            )
            return (total * factor).astype(BF)

        other = finished(oc)
        for j in range(NY):
            osd[hh, j] = other[:, j * HD : (j + 1) * HD]
        send(("ow", hh), osd.at[hh], ow.at[cc, hh], sibling)
        own = finished(cc)
        for j in range(NY):
            ow[cc, hh, j] = own[:, j * HD : (j + 1) * HD]

    def feature_term(slot):
        def body(n, carry):
            columns = pl.ds(pl.multiple_of(n * 256, 256), 256)
            total = jnp.zeros((2 * ROWS, 256), F32)
            for hh in (0, 1):
                grads = jnp.concatenate(
                    [ga[hh, j, slot].reshape(2 * ROWS, HD) for j in range(NY)], axis=1
                )
                weights = wb[hh, n].reshape(256, NY * HD)
                total += lax.dot_general(grads, weights, NT, preferred_element_type=F32)
            pieces = (total[:ROWS], total[ROWS:])
            mine = jnp.where(cc == 0, pieces[0], pieces[1])
            others = jnp.where(cc == 0, pieces[1], pieces[0])
            dk[slot, :, columns] = mine
            ds[slot, :, columns] = others.astype(BF)
            return carry

        lax.fori_loop(0, NZ, body, 0)
        send(("df", slot), ds.at[slot], dr.at[slot], sibling)

    def feature_send(slot):
        receive(("df", slot), dr.at[slot])
        dx[slot] = (dk[slot] + dr[slot].astype(F32)).astype(BF)
        send(("dx", slot), dx.at[slot], xr.at[slot], at_x(OFFSETS[slot]))

    own_weights(0)
    gather_send(0, 0)
    for slot in range(NX):
        norm_queries(slot)
    local("f", fa.at[0, cc], fa.at[0, cc]).wait()
    transpose_features(0, cc)
    gather_send(0, 1, (0,))
    receive(("fs", 0), fa.at[0, oc])
    transpose_features(0, oc)
    gather_send(0, 1, (1,))
    gather_send(0, 2, (0,))
    receive(("fx", 1), fa.at[1, cc])
    send(("fh", 0), fa.at[1, cc, pl.ds(0, 64)], fa.at[3, cc, pl.ds(0, 64)], at_x(3))
    receive(("fx", 3), fa.at[2, cc])
    send(("fh", 1), fa.at[2, cc, pl.ds(64, 64)], fa.at[3, cc, pl.ds(64, 64)], at_x(1))
    send(("fs", 1), fa.at[1, cc], fa.at[1, cc], sibling)
    send(("fs", 2), fa.at[2, cc], fa.at[2, cc], sibling)
    gather_send(0, 2, (1,))
    transpose_features(1, cc)
    transpose_features(2, cc)
    gather_send(0, 3)
    gather_rest(0)
    own_weights(1)
    gather_send(1, 0)
    receive(("fh", 0), fa.at[3, cc, pl.ds(0, 64)])
    receive(("fh", 1), fa.at[3, cc, pl.ds(64, 64)])
    send(("fs", 3), fa.at[3, cc], fa.at[3, cc], sibling)
    gather_last(0)
    receive(("fs", 1), fa.at[1, oc])
    project(0, 0)
    gather_send(1, 1, (0,))
    receive(("fs", 2), fa.at[2, oc])
    receive(("fs", 3), fa.at[3, oc])
    project(0, 1)
    gather_send(1, 1, (1,))
    transpose_features(1, oc)
    transpose_features(2, oc)
    transpose_features(3, cc)
    transpose_features(3, oc)
    for slot in range(NX):
        local(("d", slot), do.at[slot], do.at[slot]).wait()
    gather_send(1, 2, (0,))
    projected(0, 0)
    attend(0, 0)
    gather_send(1, 2, (1,))
    projected(0, 1)
    attend(0, 1)
    gather_send(1, 3)
    gather_rest(1)
    gather_last(1)
    project(1, 0)
    project(1, 1)
    gathered(0, 0)
    gathered(0, 1)
    weight_term(0, HALF)
    scatter_send(0, 0)
    for distance in (3, 5, 2, 6):
        weight_term(0, distance)
    scatter_send(0, 1)
    for distance in (1, 7, 0):
        weight_term(0, distance)
    projected(1, 0)
    attend(1, 0)
    scatter_send(0, 2)
    projected(1, 1)
    attend(1, 1)
    scatter_send(0, 3)
    scatter_last(0)
    gathered(1, 0)
    gathered(1, 1)
    weight_term(1, HALF)
    scatter_send(1, 0)
    for distance in (3, 5):
        weight_term(1, distance)
    feature_term(3)
    scatter_send(1, 1)
    feature_term(1)
    feature_send(3)
    for distance in (2, 6):
        weight_term(1, distance)
    feature_term(2)
    feature_send(1)
    scatter_send(1, 2)
    for distance in (1, 7, 0):
        weight_term(1, distance)
    feature_term(0)
    feature_send(2)
    scatter_send(1, 3)
    receive(("df", 0), dr.at[0])
    dk[0] = dk[0] + dr[0].astype(F32)
    scatter_last(1)

    for hh in (0, 1):
        receive(("ow", hh), ow.at[oc, hh])
    for kind, out in ((0, out_k), (1, out_v)):
        for hh in (0, 1):
            for j in range(NY):
                local(
                    ("out", kind, hh, j),
                    ow.at[kind, hh, j],
                    out.at[0, :, pl.ds((2 * j + hh) * HD, HD)],
                ).start()
    for slot in (1, 2, 3):
        receive(("dx", slot), xr.at[slot])
    total = dk[0]
    for slot in (1, 2, 3):
        total = total + xr[slot].astype(F32)
    dx[0] = total.astype(BF)
    local("of", dx.at[0], out_f.at[0]).start()
    for kind, out in ((0, out_k), (1, out_v)):
        for hh in (0, 1):
            for j in range(NY):
                local(
                    ("out", kind, hh, j),
                    ow.at[kind, hh, j],
                    out.at[0, :, pl.ds((2 * j + hh) * HD, HD)],
                ).wait()
    local("of", dx.at[0], out_f.at[0]).wait()
    for copy in started:
        copy.wait_send()
    assert len(ids) <= N_SEMS and len(local_ids) <= 64, (len(ids), len(local_ids))


def per_device(
    queries, grad_out, features, w_key, w_value, q_gain, k_gain, tile_counts, image_starts
):
    hbm = pl.BlockSpec(memory_space=pl.ANY)
    vmem = pl.BlockSpec(memory_space=pltpu.VMEM)
    smem = pl.BlockSpec(memory_space=pltpu.SMEM)
    flops = 3 * 2 * 512 * WIDTH * 2048 + 8 * 8 * 4 * 2 * ROWS * ROWS * HD
    return pl.pallas_call(
        kernel,
        out_shape=(
            jax.ShapeDtypeStruct((1, ROWS, WIDTH), BF),
            jax.ShapeDtypeStruct((1, ROWS, 1024), BF),
            jax.ShapeDtypeStruct((1, ROWS, 1024), BF),
        ),
        in_specs=[hbm, hbm, hbm, hbm, hbm, vmem, vmem, smem, smem],
        out_specs=(hbm, hbm, hbm),
        scratch_shapes=[
            pltpu.VMEM((4, ROWS, WIDTH), BF),
            pltpu.VMEM((4, ROWS, WIDTH), BF),
            pltpu.VMEM((4, 2, ROWS, WIDTH), BF),
            pltpu.VMEM((WIDTH, 8 * ROWS), BF),
            pltpu.VMEM((2, NZ, 2, ROWS, NY * HD), BF),
            pltpu.VMEM((2, 2, NY, 4, ROWS, HD), BF),
            pltpu.VMEM((2, 2, NY, 4, ROWS, HD), BF),
            pltpu.VMEM((2, 2, 4, ROWS, HD), BF),
            pltpu.VMEM((2, NY, 4, 2, ROWS, HD), BF),
            pltpu.VMEM((NZ, 2 * ROWS, NY * HD), F32),
            pltpu.VMEM((2, 2, HALF, 2, ROWS, NY * HD), BF),
            pltpu.VMEM((2, 2, HALF, 2, ROWS, NY * HD), BF),
            pltpu.VMEM((2, NY, ROWS, HD), BF),
            pltpu.VMEM((2, 2, NY, ROWS, HD), BF),
            pltpu.VMEM((4, ROWS, WIDTH), BF),
            pltpu.VMEM((4, ROWS, WIDTH), BF),
            pltpu.VMEM((4, ROWS, WIDTH), F32),
            pltpu.VMEM((4, ROWS, WIDTH), BF),
            pltpu.VMEM((4, ROWS, WIDTH), BF),
            pltpu.SemaphoreType.DMA((N_SEMS,)),
            pltpu.SemaphoreType.DMA((N_SEMS,)),
            pltpu.SemaphoreType.DMA((64,)),
        ],
        compiler_params=pltpu.CompilerParams(
            collective_id=0, has_side_effects=True, vmem_limit_bytes=58 << 20
        ),
        cost_estimate=pl.CostEstimate(
            flops=flops, bytes_accessed=8 << 20, transcendentals=1 << 20
        ),
        name="cross_attention_backward",
    )(queries, grad_out, features, w_key, w_value, q_gain, k_gain, tile_counts, image_starts)


def solution(mesh):
    in_specs = (
        P("pipe", None, "dp", "mp"),
        P("pipe", None, "dp", "mp"),
        P("pipe", "dp", "mp"),
        P("pipe", ("mp", "dp"), None),
        P("pipe", ("mp", "dp"), None),
        P("pipe", None),
        P("pipe", None),
        P(None, "dp", None),
        P(None, "dp", None),
    )
    out_specs = (
        P("pipe", "dp", "mp"),
        P("pipe", ("mp", "dp"), None),
        P("pipe", ("mp", "dp"), None),
    )
    return jax.shard_map(
        per_device, mesh=mesh, in_specs=in_specs, out_specs=out_specs, check_vma=False
    )
```

```python
import math

import jax
import jax.numpy as jnp
from jax import lax
from jax.experimental import pallas as pl
from jax.experimental.pallas import tpu as pltpu
from jax.sharding import PartitionSpec as P

TILE_TOK = 16
EPSILON = 1e-05
NX, NY, NZ = 4, 4, 8
HD = 128
ROWS = 128
WIDTH = 2048
GROUPS = 8
OFFSETS = (0, 1, 3, 2)
RIGHT, LEFT = 0, 1
HALF = NZ // 2
BF = jnp.bfloat16
F32 = jnp.float32
MESH = pl.DeviceIdType.MESH
N_SEMS = 224
NT = (((1,), (1,)), ((), ()))


def kernel(
    queries,
    grad_out,
    features,
    w_key,
    w_value,
    q_gain,
    k_gain,
    tiles,
    starts,
    out_f,
    out_k,
    out_v,
    qb,
    do,
    fa,
    ft,
    wb,
    ps,
    rk,
    kh,
    gs,
    ga,
    pw,
    sb,
    rb,
    osd,
    ow,
    ds,
    dr,
    af,
    dx,
    xh,
    xr,
    send_sems,
    recv_sems,
    local_sems,
):
    px = lax.axis_index("pipe")
    dd = lax.axis_index("dp")
    qy = lax.axis_index("mp")
    zz = dd // 2
    cc = dd % 2
    oc = 1 - cc
    kinds = (w_key, w_value)

    def at_x(step):
        return ((px + step) % NX, dd, qy)

    def at_y(step, core):
        return (px, zz * 2 + core, (qy + step) % NY)

    def at_z(step):
        return (px, ((zz + step) % NZ) * 2 + cc, qy)

    sibling = (px, zz * 2 + oc, qy)

    ids = {}
    started = []

    def sem_of(key):
        return ids.setdefault(key, len(ids))

    def remote(key, src, dst, device):
        n = sem_of(key)
        return pltpu.make_async_remote_copy(
            src_ref=src,
            dst_ref=dst,
            send_sem=send_sems.at[n],
            recv_sem=recv_sems.at[n],
            device_id=device,
            device_id_type=MESH,
        )

    def send(key, src, dst, device):
        copy = remote(key, src, dst, device)
        copy.start()
        started.append(copy)
        return copy

    def receive(key, dst):
        remote(key, dst, dst, sibling).wait_recv()

    local_ids = {}

    def local(key, src, dst):
        n = local_ids.setdefault(key, len(local_ids))
        return pltpu.make_async_copy(src, dst, local_sems.at[n])

    barrier = pltpu.get_barrier_semaphore()
    partners = [sibling, at_z(1), at_z(NZ - 1)]
    partners += [at_x(step) for step in (1, 3)]
    partners += [at_y(step, core) for step in (1, 3) for core in (cc, oc)]
    for device in partners:
        pl.semaphore_signal(barrier, inc=1, device_id=device, device_id_type=MESH)

    def weight_columns(ref, hh, j):
        return ref.at[0, :, pl.ds((2 * j + hh) * HD, HD)]

    for kind in (0, 1):

        @pl.when(cc == kind)
        def _():
            for hh in (0, 1):
                for j in range(NY):
                    local(
                        ("w", hh, j),
                        weight_columns(kinds[kind], hh, j),
                        wb.at[hh, zz, cc, :, pl.ds(j * HD, HD)],
                    ).start()

    local("f", features.at[0], fa.at[0, cc]).start()
    for slot in range(NX):
        local(("q", slot), queries.at[0, (px + OFFSETS[slot]) % NX], qb.at[slot]).start()
        local(("d", slot), grad_out.at[0, (px + OFFSETS[slot]) % NX], do.at[slot]).start()

    pl.semaphore_wait(barrier, len(partners))

    for kind in (0, 1):

        @pl.when(oc == kind)
        def _():
            for hh in (0, 1):
                for j in range(NY):
                    remote(
                        ("w", hh, j),
                        weight_columns(kinds[kind], hh, j),
                        wb.at[hh, zz, cc, :, pl.ds(j * HD, HD)],
                        sibling,
                    ).start()

    for hh in (0, 1):
        for j in range(NY):
            piece = wb.at[hh, zz, cc, :, pl.ds(j * HD, HD)]
            started.append(remote(("w", hh, j), piece, piece, sibling))

    send(("fx", 3), features.at[0], fa.at[2, cc], at_x(1))
    send(("fx", 1), features.at[0], fa.at[1, cc], at_x(3))
    send(("fs", 0), features.at[0], fa.at[0, cc], sibling)

    def origin(direction, k):
        return (zz - k + NZ) % NZ if direction == RIGHT else (zz + k) % NZ

    def onward(direction):
        return at_z(1 if direction == RIGHT else NZ - 1)

    in_flight = {}

    def sent(key):
        for copy in in_flight.pop(key):
            copy.wait_send()
            started[:] = [other for other in started if other is not copy]

    def gather(hh, n):
        k, second = n // 2, n % 2
        in_flight["ag", hh, n] = copies = []
        for direction in (RIGHT, LEFT):
            piece = 1 - direction if second else direction
            block = wb.at[hh, origin(direction, k), piece]
            if k:
                receive(("ag", direction, hh, k - 1, piece), block)
            copies.append(
                send(("ag", direction, hh, k, piece), block, block, onward(direction))
            )

    def gather_done(hh):
        for k, second in ((HALF - 2, 1), (HALF - 1, 0)):
            for direction in (RIGHT, LEFT):
                piece = 1 - direction if second else direction
                receive(
                    ("ag", direction, hh, k, piece),
                    wb.at[hh, origin(direction, k + 1), piece],
                )

    def own_weights(hh):
        for j in range(NY):
            piece = wb.at[hh, zz, cc, :, pl.ds(j * HD, HD)]
            local(("w", hh, j), piece, piece).wait()
        for j in range(NY):
            piece = wb.at[hh, zz, oc, :, pl.ds(j * HD, HD)]
            receive(("w", hh, j), piece)

    def norm_queries(slot):
        local(("q", slot), qb.at[slot], qb.at[slot]).wait()
        gain = q_gain[...]

        def body(i, carry):
            for u in range(4):
                columns = pl.ds(pl.multiple_of((i * 4 + u) * HD, HD), HD)
                values = qb[slot, :, columns].astype(F32)
                inverse = lax.rsqrt(
                    jnp.mean(values * values, axis=-1, keepdims=True) + EPSILON
                )
                qb[slot, :, columns] = (values * inverse * gain).astype(BF)
            return carry

        lax.fori_loop(0, WIDTH // HD // 4, body, 0)

    def transpose_features(slot, replica):
        place = pl.multiple_of((slot * 2 + replica) * ROWS, ROWS)

        def body(i, carry):
            for u in range(2):
                columns = pl.ds(pl.multiple_of((i * 2 + u) * HD, HD), HD)
                ft[columns, pl.ds(place, ROWS)] = fa[slot, replica, :, columns].T
            return carry

        lax.fori_loop(0, WIDTH // HD // 2, body, 0)

    def project(hh, mg):
        def body(n, carry):
            rows = fa[2 * mg : 2 * mg + 2].reshape(4 * ROWS, WIDTH)
            columns = pl.ds(pl.multiple_of(n * 256, 256), 256)
            weights = wb[hh, :, :, :, columns].reshape(WIDTH, 256)
            total = jnp.dot(rows, weights, preferred_element_type=F32).astype(BF)
            for slot in (0, 1):
                for replica in (0, 1):
                    low = (slot * 2 + replica) * ROWS
                    for j in (0, 1):
                        ps[hh, replica, n * 2 + j, 2 * mg + slot] = total[
                            low : low + ROWS, j * HD : (j + 1) * HD
                        ]
            return carry

        lax.fori_loop(0, 2, body, 0)
        far = (qy + 2) % NY
        for way, slot in ((RIGHT, 2 * mg), (LEFT, 2 * mg + 1)):
            send(
                ("kh", hh, mg, way),
                ps.at[hh, :, far, slot],
                kh.at[hh, mg, way],
                at_y(1 if way == RIGHT else 3, cc),
            )
        for way, slot in ((RIGHT, 2 * mg + 1), (LEFT, 2 * mg)):
            send_keys(hh, way, slot)
        pair = pl.ds(2 * mg, 2)
        send(("kv", hh, mg), ps.at[hh, oc, qy, pair], rk.at[hh, cc, 0, pair], sibling)
        local(("kv", hh, mg), ps.at[hh, cc, qy, pair], rk.at[hh, cc, 0, pair]).start()

    def send_keys(hh, way, slot):
        step = 1 if way == RIGHT else 3
        for same in (1, 0):
            core = cc if same else oc
            send(
                ("ky", hh, way, slot, same),
                ps.at[hh, core, (qy + step) % NY, slot],
                rk.at[hh, cc, 1 + way, slot],
                at_y(step, core),
            )

    def relay_keys(hh, mg):
        for way, slot in ((RIGHT, 2 * mg), (LEFT, 2 * mg + 1)):
            target = (qy + (1 if way == RIGHT else 3)) % NY
            receive(("kh", hh, mg, way), kh.at[hh, mg, way])
            for replica in (0, 1):
                ps[hh, replica, target, slot] = (
                    ps[hh, replica, target, slot].astype(F32)
                    + kh[hh, mg, way, replica].astype(F32)
                ).astype(BF)
            send_keys(hh, way, slot)

    def projected(hh, mg):
        pair = pl.ds(2 * mg, 2)
        local(("kv", hh, mg), rk.at[hh, cc, 0, pair], rk.at[hh, cc, 0, pair]).wait()
        receive(("kv", hh, mg), rk.at[hh, oc, 0, pair])
        for way in (RIGHT, LEFT):
            for slot in (2 * mg, 2 * mg + 1):
                for same in (1, 0):
                    receive(
                        ("ky", hh, way, slot, same),
                        rk.at[hh, cc if same else oc, 1 + way, slot],
                    )

    root_scale = 1.0 / math.sqrt(HD)

    def attend(hh, mg):
        gain = k_gain[...]

        def body(i, carry):
            slot = 2 * mg + i
            micro = (px + i) % NX if mg == 0 else (px + 3 - i) % NX
            key_pre = rk[hh, 0, 0, slot].astype(F32)
            value = rk[hh, 1, 0, slot].astype(F32)
            for step in (1, 2):
                key_pre += rk[hh, 0, step, slot].astype(F32)
                value += rk[hh, 1, step, slot].astype(F32)
            value = value.astype(BF)
            inverse = lax.rsqrt(
                jnp.mean(key_pre * key_pre, axis=-1, keepdims=True) + EPSILON
            )
            key = (key_pre * inverse * gain).astype(BF)
            slots = lax.broadcasted_iota(jnp.int32, (ROWS, 2 * ROWS), 0)
            texts = lax.broadcasted_iota(jnp.int32, (ROWS, 2 * ROWS), 1) % ROWS
            first = tiles[0, 0, micro] * TILE_TOK
            second = first + tiles[0, 1, micro] * TILE_TOK
            seen = ((slots < first) & (texts >= starts[0, 0, micro])) | (
                (slots >= first) & (slots < second) & (texts >= starts[0, 1, micro])
            )
            visible = jnp.where(seen, 1.0, 0.0).astype(F32)
            value_grad = jnp.zeros((ROWS, HD), F32)
            normed_grad = jnp.zeros((ROWS, HD), F32)
            for g in range(0, GROUPS, 2):
                low = (hh * GROUPS + g) * HD
                query = jnp.concatenate(
                    [qb[slot, :, low : low + HD], qb[slot, :, low + HD : low + 2 * HD]], axis=0
                )
                grad = jnp.concatenate(
                    [do[slot, :, low : low + HD], do[slot, :, low + HD : low + 2 * HD]], axis=0
                )
                scores = (
                    lax.dot_general(key, query, NT, preferred_element_type=F32) * root_scale
                )
                weights = jnp.exp(scores) * visible
                total = jnp.sum(weights, axis=0, keepdims=True)
                probability = weights * (1.0 / jnp.where(total > 0, total, 1.0))
                prob_grad = lax.dot_general(value, grad, NT, preferred_element_type=F32)
                delta = jnp.sum(probability * prob_grad, axis=0, keepdims=True)
                score_grad = (probability * (prob_grad - delta)).astype(BF)
                value_grad += jnp.dot(
                    probability.astype(BF), grad, preferred_element_type=F32
                )
                normed_grad += jnp.dot(score_grad, query, preferred_element_type=F32)
            scaled = normed_grad * root_scale * gain
            key_grad = inverse * scaled - key_pre * (inverse * inverse * inverse) * jnp.mean(
                scaled * key_pre, axis=-1, keepdims=True
            )
            gs[hh, 0, slot] = key_grad.astype(BF)
            gs[hh, 1, slot] = value_grad.astype(BF)
            return carry

        lax.fori_loop(0, 2, body, 0)
        pair = pl.ds(2 * mg, 2)
        for step in (1, 3, 0):
            for same in (1, 0):
                kind = cc if same else oc
                src = gs.at[hh, kind, pair]
                dst = ga.at[hh, qy, pair, cc]
                if step == 0 and same:
                    local(("g", hh, mg), src, dst).start()
                else:
                    send(("g", hh, mg, step, same), src, dst, at_y(step, kind))

    def relay_grads(hh, mg):
        for step, slot in ((1, 2 * mg), (3, 2 * mg + 1)):
            source = (qy - step + NY) % NY
            for same in (1, 0):
                receive(
                    ("g", hh, mg, step, same),
                    ga.at[hh, source, pl.ds(2 * mg, 2), cc if same else oc],
                )
            block = ga.at[hh, source, slot]
            send(("gh", hh, mg, step), block, block, at_y(step, cc))

    def gathered(hh, mg):
        pair = pl.ds(2 * mg, 2)
        dst = ga.at[hh, qy, pair, cc]
        local(("g", hh, mg), dst, dst).wait()
        receive(("g", hh, mg, 0, 0), ga.at[hh, qy, pair, oc])
        for step, slot in ((1, 2 * mg), (3, 2 * mg + 1)):
            receive(("gh", hh, mg, step), ga.at[hh, (qy + 2) % NY, slot])

    def weight_term(hh, distance):
        block = (zz + distance) % NZ
        lhs = ft[pl.ds(pl.multiple_of(block * 256, 256), 256), :]

        def body(n, carry):
            columns = pl.ds(pl.multiple_of(n * 256, 256), 256)
            grads = jnp.concatenate(
                [ga[hh, n * 2 + j].reshape(8 * ROWS, HD) for j in (0, 1)], axis=1
            )
            pw[hh, distance, :, columns] = jnp.dot(lhs, grads, preferred_element_type=F32)
            return carry

        lax.fori_loop(0, 2, body, 0)

    def scatter(hh, n):
        k, second = (n + 1) // 2, n % 2
        in_flight["rs", hh, n] = copies = []
        for direction in (RIGHT, LEFT):
            piece = 1 - direction if second else direction
            distance = HALF - k if direction == RIGHT else HALF + k
            total = pw[hh, distance, piece * ROWS : (piece + 1) * ROWS, :]
            if n > 1:
                arrived = rb.at[hh, direction, k - 1, piece]
                receive(("rs", direction, hh, k - 1, piece), arrived)
                total = total + arrived[...].astype(F32)
            sb[hh, direction, k, piece] = total.astype(BF)
            copies.append(
                send(
                    ("rs", direction, hh, k, piece),
                    sb.at[hh, direction, k, piece],
                    rb.at[hh, direction, k, piece],
                    onward(direction),
                )
            )

    factor = 1.0 / (NX * NZ * 2)

    def scatter_done(hh):
        for direction in (RIGHT, LEFT):
            for piece in (0, 1):
                receive(
                    ("rs", direction, hh, HALF - 1, piece), rb.at[hh, direction, HALF - 1, piece]
                )

        def finished(piece):
            total = (
                pw[hh, 0, pl.ds(pl.multiple_of(piece * ROWS, ROWS), ROWS), :]
                + rb[hh, RIGHT, HALF - 1, piece].astype(F32)
                + rb[hh, LEFT, HALF - 1, piece].astype(F32)
            )
            return (total * factor).astype(BF)

        other = finished(oc)
        for j in range(NY):
            osd[hh, j] = other[:, j * HD : (j + 1) * HD]
        send(("ow", hh), osd.at[hh], ow.at[cc, hh], sibling)
        own = finished(cc)
        for j in range(NY):
            ow[cc, hh, j] = own[:, j * HD : (j + 1) * HD]

    def feature_term(hh, pair):
        def body(n, carry):
            columns = pl.ds(pl.multiple_of(n * 256, 256), 256)
            grads = jnp.concatenate(
                [ga[hh, j, 2 * pair : 2 * pair + 2].reshape(4 * ROWS, HD) for j in range(NY)],
                axis=1,
            )
            weights = wb[hh, n].reshape(256, NY * HD)
            total = lax.dot_general(grads, weights, NT, preferred_element_type=F32)
            for i in (0, 1):
                slot = 2 * pair + i
                terms = [total[(2 * i + r) * ROWS : (2 * i + r + 1) * ROWS] for r in (0, 1)]
                if hh == 0:
                    for r in (0, 1):
                        af[slot, r, :, columns] = terms[r]
                else:
                    terms = [terms[r] + af[slot, r, :, columns] for r in (0, 1)]
                    af[slot, 0, :, columns] = jnp.where(cc == 0, terms[0], terms[1])
                    ds[slot, :, columns] = jnp.where(cc == 0, terms[1], terms[0]).astype(BF)
            return carry

        lax.fori_loop(0, NZ, body, 0)
        if hh == 1:
            for slot in (2 * pair + 1, 2 * pair):
                send(("df", slot), ds.at[slot], dr.at[slot], sibling)

    half = ROWS // 2

    def feature_far():
        receive(("df", 3), dr.at[3])
        dx[3] = (af[3, 0] + dr[3].astype(F32)).astype(BF)
        for way in (RIGHT, LEFT):
            send(
                ("xh", way),
                dx.at[3, pl.ds(way * half, half)],
                xh.at[way],
                at_x(1 if way == RIGHT else 3),
            )

    def feature_send(way, second):
        slot = 1 if way == RIGHT else 2
        low = half * (way if second else 1 - way)
        total = af[slot, 0, low : low + half] + dr[slot, low : low + half].astype(F32)
        if second:
            receive(("xh", way), xh.at[way])
            total = total + xh[way].astype(F32)
        dx[slot, low : low + half] = total.astype(BF)
        rows = pl.ds(low, half)
        send(
            ("xr", way, second),
            dx.at[slot, rows],
            xr.at[way, rows],
            at_x(1 if way == RIGHT else 3),
        )

    own_weights(0)
    gather(0, 0)
    norm_queries(0)
    sent(("ag", 0, 0))
    gather(0, 1)
    norm_queries(1)
    gather(0, 2)
    norm_queries(2)
    gather(0, 3)
    norm_queries(3)
    local("f", fa.at[0, cc], fa.at[0, cc]).wait()
    transpose_features(0, cc)
    gather(0, 4)
    receive(("fs", 0), fa.at[0, oc])
    transpose_features(0, oc)
    gather(0, 5)
    receive(("fx", 1), fa.at[1, cc])
    send(("fh", 0), fa.at[1, cc, pl.ds(0, 64)], fa.at[3, cc, pl.ds(0, 64)], at_x(3))
    receive(("fx", 3), fa.at[2, cc])
    send(("fh", 1), fa.at[2, cc, pl.ds(64, 64)], fa.at[3, cc, pl.ds(64, 64)], at_x(1))
    send(("fs", 1), fa.at[1, cc], fa.at[1, cc], sibling)
    send(("fs", 2), fa.at[2, cc], fa.at[2, cc], sibling)
    own_weights(1)
    gather(0, 6)
    transpose_features(1, cc)
    transpose_features(2, cc)
    sent(("ag", 0, 5))
    gather(1, 0)
    receive(("fh", 0), fa.at[3, cc, pl.ds(0, 64)])
    receive(("fh", 1), fa.at[3, cc, pl.ds(64, 64)])
    send(("fs", 3), fa.at[3, cc], fa.at[3, cc], sibling)
    sent(("ag", 0, 6))
    gather(1, 1)
    gather_done(0)
    receive(("fs", 1), fa.at[1, oc])
    project(0, 0)
    gather(1, 2)
    receive(("fs", 2), fa.at[2, oc])
    receive(("fs", 3), fa.at[3, oc])
    project(0, 1)
    gather(1, 3)
    transpose_features(1, oc)
    relay_keys(0, 0)
    transpose_features(2, oc)
    relay_keys(0, 1)
    gather(1, 4)
    transpose_features(3, cc)
    transpose_features(3, oc)
    for slot in range(NX):
        local(("d", slot), do.at[slot], do.at[slot]).wait()
    projected(0, 0)
    attend(0, 0)
    gather(1, 5)
    projected(0, 1)
    attend(0, 1)
    gather(1, 6)
    relay_grads(0, 0)
    relay_grads(0, 1)
    gather_done(1)
    project(1, 0)
    project(1, 1)
    gathered(0, 0)
    gathered(0, 1)
    weight_term(0, 4)
    scatter(0, 0)
    weight_term(0, 3)
    weight_term(0, 5)
    sent(("rs", 0, 0))
    scatter(0, 1)
    relay_keys(1, 0)
    relay_keys(1, 1)
    weight_term(0, 2)
    weight_term(0, 6)
    scatter(0, 2)
    for distance in (1, 7, 0):
        weight_term(0, distance)
    scatter(0, 3)
    projected(1, 0)
    attend(1, 0)
    scatter(0, 4)
    projected(1, 1)
    attend(1, 1)
    scatter(0, 5)
    relay_grads(1, 0)
    feature_term(0, 1)
    scatter(0, 6)
    relay_grads(1, 1)
    feature_term(0, 0)
    gathered(1, 0)
    gathered(1, 1)
    weight_term(1, 4)
    scatter(1, 0)
    weight_term(1, 3)
    weight_term(1, 5)
    scatter(1, 1)
    feature_term(1, 1)
    scatter(1, 2)
    for distance in (2, 6):
        weight_term(1, distance)
    feature_far()
    scatter(1, 3)
    receive(("df", 2), dr.at[2])
    feature_send(LEFT, 0)
    feature_term(1, 0)
    scatter(1, 4)
    receive(("df", 1), dr.at[1])
    feature_send(RIGHT, 0)
    for distance in (1, 7, 0):
        weight_term(1, distance)
    scatter(1, 5)
    feature_send(LEFT, 1)
    feature_send(RIGHT, 1)
    scatter_done(0)
    receive(("df", 0), dr.at[0])
    scatter(1, 6)
    scatter_done(1)

    for hh in (0, 1):
        receive(("ow", hh), ow.at[oc, hh])
    for kind, out in ((0, out_k), (1, out_v)):
        for hh in (0, 1):
            for j in range(NY):
                local(
                    ("out", kind, hh, j),
                    ow.at[kind, hh, j],
                    out.at[0, :, pl.ds((2 * j + hh) * HD, HD)],
                ).start()
    for way in (RIGHT, LEFT):
        for second in (0, 1):
            low = half * (way if second else 1 - way)
            receive(("xr", way, second), xr.at[way, pl.ds(low, half)])
    total = af[0, 0] + dr[0].astype(F32)
    for way in (RIGHT, LEFT):
        total = total + xr[way].astype(F32)
    dx[0] = total.astype(BF)
    local("of", dx.at[0], out_f.at[0]).start()
    for kind, out in ((0, out_k), (1, out_v)):
        for hh in (0, 1):
            for j in range(NY):
                local(
                    ("out", kind, hh, j),
                    ow.at[kind, hh, j],
                    out.at[0, :, pl.ds((2 * j + hh) * HD, HD)],
                ).wait()
    local("of", dx.at[0], out_f.at[0]).wait()
    for copy in started:
        copy.wait_send()
    assert len(ids) <= N_SEMS and len(local_ids) <= 64, (len(ids), len(local_ids))


def copy_results(a, b, c, x, y, z, hold_a, hold_b, hold_c, sems):
    parts = ((a, hold_a, x), (b, hold_b, y), (c, hold_c, z))
    reads = [pltpu.make_async_copy(p[0], p[1], sems.at[n]) for n, p in enumerate(parts)]
    writes = [pltpu.make_async_copy(p[1], p[2], sems.at[3 + n]) for n, p in enumerate(parts)]
    for copy in reads:
        copy.start()
    for n in range(3):
        reads[n].wait()
        writes[n].start()
    for copy in writes:
        copy.wait()


def per_device(
    queries, grad_out, features, w_key, w_value, q_gain, k_gain, tile_counts, image_starts
):
    hbm = pl.BlockSpec(memory_space=pl.ANY)
    vmem = pl.BlockSpec(memory_space=pltpu.VMEM)
    smem = pl.BlockSpec(memory_space=pltpu.SMEM)
    tiles = jnp.transpose(tile_counts, (1, 2, 0))
    starts = jnp.transpose(image_starts, (1, 2, 0))
    flops = 3 * 2 * 512 * WIDTH * 2048 + 8 * 8 * 4 * 2 * ROWS * ROWS * HD
    results = pl.pallas_call(
        kernel,
        out_shape=(
            jax.ShapeDtypeStruct((1, ROWS, WIDTH), BF),
            jax.ShapeDtypeStruct((1, ROWS, 1024), BF),
            jax.ShapeDtypeStruct((1, ROWS, 1024), BF),
        ),
        in_specs=[hbm, hbm, hbm, hbm, hbm, vmem, vmem, smem, smem],
        out_specs=(hbm, hbm, hbm),
        scratch_shapes=[
            pltpu.VMEM((4, ROWS, WIDTH), BF),
            pltpu.VMEM((4, ROWS, WIDTH), BF),
            pltpu.VMEM((4, 2, ROWS, WIDTH), BF),
            pltpu.VMEM((WIDTH, 8 * ROWS), BF),
            pltpu.VMEM((2, NZ, 2, ROWS, NY * HD), BF),
            pltpu.VMEM((2, 2, NY, 4, ROWS, HD), BF),
            pltpu.VMEM((2, 2, 3, 4, ROWS, HD), BF),
            pltpu.VMEM((2, 2, 2, 2, ROWS, HD), BF),
            pltpu.VMEM((2, 2, 4, ROWS, HD), BF),
            pltpu.VMEM((2, NY, 4, 2, ROWS, HD), BF),
            pltpu.VMEM((2, NZ, 2 * ROWS, NY * HD), F32),
            pltpu.VMEM((2, 2, HALF, 2, ROWS, NY * HD), BF),
            pltpu.VMEM((2, 2, HALF, 2, ROWS, NY * HD), BF),
            pltpu.VMEM((2, NY, ROWS, HD), BF),
            pltpu.VMEM((2, 2, NY, ROWS, HD), BF),
            pltpu.VMEM((4, ROWS, WIDTH), BF),
            pltpu.VMEM((4, ROWS, WIDTH), BF),
            pltpu.VMEM((4, 2, ROWS, WIDTH), F32),
            pltpu.VMEM((4, ROWS, WIDTH), BF),
            pltpu.VMEM((2, 64, WIDTH), BF),
            pltpu.VMEM((2, ROWS, WIDTH), BF),
            pltpu.SemaphoreType.DMA((N_SEMS,)),
            pltpu.SemaphoreType.DMA((N_SEMS,)),
            pltpu.SemaphoreType.DMA((64,)),
        ],
        compiler_params=pltpu.CompilerParams(
            collective_id=0, has_side_effects=True, vmem_limit_bytes=58 << 20
        ),
        cost_estimate=pl.CostEstimate(
            flops=flops, bytes_accessed=8 << 20, transcendentals=1 << 20
        ),
        name="cross_attention_backward",
    )(queries, grad_out, features, w_key, w_value, q_gain, k_gain, tiles, starts)
    return pl.pallas_call(
        copy_results,
        out_shape=tuple(jax.ShapeDtypeStruct(r.shape, r.dtype) for r in results),
        in_specs=[hbm, hbm, hbm],
        out_specs=(hbm, hbm, hbm),
        scratch_shapes=[pltpu.VMEM(r.shape, r.dtype) for r in results]
        + [pltpu.SemaphoreType.DMA((6,))],
        name="copy_results",
    )(*results)


def solution(mesh):
    in_specs = (
        P("pipe", None, "dp", "mp"),
        P("pipe", None, "dp", "mp"),
        P("pipe", "dp", "mp"),
        P("pipe", ("mp", "dp"), None),
        P("pipe", ("mp", "dp"), None),
        P("pipe", None),
        P("pipe", None),
        P(None, "dp", None),
        P(None, "dp", None),
    )
    out_specs = (
        P("pipe", "dp", "mp"),
        P("pipe", ("mp", "dp"), None),
        P("pipe", ("mp", "dp"), None),
    )
    return jax.shard_map(
        per_device, mesh=mesh, in_specs=in_specs, out_specs=out_specs, check_vma=False
    )
```

```python
import math

import jax
import jax.numpy as jnp
from jax import lax
from jax.experimental import pallas as pl
from jax.experimental.pallas import tpu as pltpu
from jax.sharding import PartitionSpec as P

TILE_TOK = 16
EPSILON = 1e-05
NX, NY, NZ = 4, 4, 8
HD = 128
ROWS = 128
WIDTH = 2048
GROUPS = 8
OFFSETS = (0, 1, 3, 2)
RIGHT, LEFT = 0, 1
HALF = NZ // 2
BF = jnp.bfloat16
F32 = jnp.float32
MESH = pl.DeviceIdType.MESH
N_SEMS = 224
NT = (((1,), (1,)), ((), ()))


def kernel(
    queries,
    grad_out,
    features,
    w_key,
    w_value,
    q_gain,
    k_gain,
    tiles,
    starts,
    out_f,
    out_k,
    out_v,
    qb,
    do,
    fa,
    ft,
    wb,
    ps,
    rk,
    kh,
    gs,
    ga,
    pw,
    sb,
    rb,
    osd,
    ow,
    ds,
    dr,
    af,
    dx,
    xh,
    xr,
    send_sems,
    recv_sems,
    local_sems,
):
    px = lax.axis_index("pipe")
    dd = lax.axis_index("dp")
    qy = lax.axis_index("mp")
    zz = dd // 2
    cc = dd % 2
    oc = 1 - cc
    kinds = (w_key, w_value)

    def at_x(step):
        return ((px + step) % NX, dd, qy)

    def at_y(step, core):
        return (px, zz * 2 + core, (qy + step) % NY)

    def at_z(step):
        return (px, ((zz + step) % NZ) * 2 + cc, qy)

    sibling = (px, zz * 2 + oc, qy)

    ids = {}
    started = []

    def sem_of(key):
        return ids.setdefault(key, len(ids))

    def remote(key, src, dst, device):
        n = sem_of(key)
        return pltpu.make_async_remote_copy(
            src_ref=src,
            dst_ref=dst,
            send_sem=send_sems.at[n],
            recv_sem=recv_sems.at[n],
            device_id=device,
            device_id_type=MESH,
        )

    def send(key, src, dst, device):
        copy = remote(key, src, dst, device)
        copy.start()
        started.append(copy)
        return copy

    waited = set()

    def receive(key, dst):
        if key not in waited:
            waited.add(key)
            remote(key, dst, dst, sibling).wait_recv()

    local_ids = {}

    def local(key, src, dst):
        n = local_ids.setdefault(key, len(local_ids))
        return pltpu.make_async_copy(src, dst, local_sems.at[n])

    def loaded(key, dst):
        if key not in waited:
            waited.add(key)
            local(key, dst, dst).wait()

    barrier = pltpu.get_barrier_semaphore()
    partners = [sibling, at_z(1), at_z(NZ - 1)]
    partners += [at_x(step) for step in (1, 3)]
    partners += [at_y(step, core) for step in (1, 3) for core in (cc, oc)]
    for device in partners:
        pl.semaphore_signal(barrier, inc=1, device_id=device, device_id_type=MESH)

    def weight_columns(ref, hh, j):
        return ref.at[0, :, pl.ds((2 * j + hh) * HD, HD)]

    for kind in (0, 1):

        @pl.when(cc == kind)
        def _():
            for hh in (0, 1):
                for j in range(NY):
                    local(
                        ("lw", hh, j),
                        weight_columns(kinds[kind], hh, j),
                        wb.at[hh, zz, cc, :, pl.ds(j * HD, HD)],
                    ).start()

    local("f", features.at[0], fa.at[0, cc]).start()
    for slot in range(NX):
        local(("q", slot), queries.at[0, (px + OFFSETS[slot]) % NX], qb.at[slot]).start()
        local(("d", slot), grad_out.at[0, (px + OFFSETS[slot]) % NX], do.at[slot]).start()

    pl.semaphore_wait(barrier, len(partners))

    for kind in (0, 1):

        @pl.when(oc == kind)
        def _():
            for hh in (0, 1):
                for j in range(NY):
                    remote(
                        ("w", hh, j),
                        weight_columns(kinds[kind], hh, j),
                        wb.at[hh, zz, cc, :, pl.ds(j * HD, HD)],
                        sibling,
                    ).start()

    for hh in (0, 1):
        for j in range(NY):
            piece = wb.at[hh, zz, cc, :, pl.ds(j * HD, HD)]
            started.append(remote(("w", hh, j), piece, piece, sibling))

    send(("fx", 3), features.at[0], fa.at[2, cc], at_x(1))
    send(("fx", 1), features.at[0], fa.at[1, cc], at_x(3))
    send(("fs", 0), features.at[0], fa.at[0, cc], sibling)

    def origin(direction, k):
        return (zz - k + NZ) % NZ if direction == RIGHT else (zz + k) % NZ

    def onward(direction):
        return at_z(1 if direction == RIGHT else NZ - 1)

    in_flight = {}

    def sent(key):
        for copy in in_flight.pop(key):
            copy.wait_send()
            started[:] = [other for other in started if other is not copy]

    def gather(hh, n):
        k, second = n // 2, n % 2
        if n == 0:
            own_weights(hh)
        before = {(0, 1): (0, 0), (1, 0): (0, 5), (1, 1): (0, 6)}.get((hh, n))
        if before:
            sent(("ag", *before))
        in_flight["ag", hh, n] = copies = []
        for direction in (RIGHT, LEFT):
            piece = 1 - direction if second else direction
            block = wb.at[hh, origin(direction, k), piece]
            if k:
                receive(("ag", direction, hh, k - 1, piece), block)
            copies.append(
                send(("ag", direction, hh, k, piece), block, block, onward(direction))
            )

    def gather_done(hh):
        for k, second in ((HALF - 2, 1), (HALF - 1, 0)):
            for direction in (RIGHT, LEFT):
                piece = 1 - direction if second else direction
                receive(
                    ("ag", direction, hh, k, piece),
                    wb.at[hh, origin(direction, k + 1), piece],
                )

    def own_weights(hh):
        for j in range(NY):
            piece = wb.at[hh, zz, cc, :, pl.ds(j * HD, HD)]
            loaded(("lw", hh, j), piece)
        for j in range(NY):
            piece = wb.at[hh, zz, oc, :, pl.ds(j * HD, HD)]
            receive(("w", hh, j), piece)

    def norm_queries(slot):
        loaded(("q", slot), qb.at[slot])
        gain = q_gain[...]

        def body(i, carry):
            for u in range(4):
                columns = pl.ds(pl.multiple_of((i * 4 + u) * HD, HD), HD)
                values = qb[slot, :, columns].astype(F32)
                inverse = lax.rsqrt(
                    jnp.mean(values * values, axis=-1, keepdims=True) + EPSILON
                )
                qb[slot, :, columns] = (values * inverse * gain).astype(BF)
            return carry

        lax.fori_loop(0, WIDTH // HD // 4, body, 0)

    def features_ready(slot, same):
        block = fa.at[slot, cc if same else oc]
        if not same:
            receive(("fs", slot), block)
        elif slot == 0:
            loaded("f", block)
        elif slot == 3:
            for way in (0, 1):
                receive(("fh", way), fa.at[3, cc, pl.ds(way * 64, 64)])
        else:
            receive(("fx", 1 if slot == 1 else 3), block)

    def relay_features(way):
        slot, rows = 1 + way, pl.ds(way * 64, 64)
        features_ready(slot, 1)
        send(("fh", way), fa.at[slot, cc, rows], fa.at[3, cc, rows], at_x(3 if way == 0 else 1))
        send(("fs", slot), fa.at[slot, cc], fa.at[slot, cc], sibling)

    def far_features():
        features_ready(3, 1)
        send(("fs", 3), fa.at[3, cc], fa.at[3, cc], sibling)

    def transpose_features(slot, same):
        features_ready(slot, same)
        replica = cc if same else oc
        place = pl.multiple_of((slot * 2 + replica) * ROWS, ROWS)

        def body(i, carry):
            for u in range(2):
                columns = pl.ds(pl.multiple_of((i * 2 + u) * HD, HD), HD)
                ft[columns, pl.ds(place, ROWS)] = fa[slot, replica, :, columns].T
            return carry

        lax.fori_loop(0, WIDTH // HD // 2, body, 0)

    def project(hh, mg):
        gather_done(hh)
        for slot in (2 * mg, 2 * mg + 1):
            for same in (1, 0):
                features_ready(slot, same)

        def body(n, carry):
            rows = fa[2 * mg : 2 * mg + 2].reshape(4 * ROWS, WIDTH)
            columns = pl.ds(pl.multiple_of(n * 256, 256), 256)
            weights = wb[hh, :, :, :, columns].reshape(WIDTH, 256)
            total = jnp.dot(rows, weights, preferred_element_type=F32).astype(BF)
            for slot in (0, 1):
                for replica in (0, 1):
                    low = (slot * 2 + replica) * ROWS
                    for j in (0, 1):
                        ps[hh, replica, n * 2 + j, 2 * mg + slot] = total[
                            low : low + ROWS, j * HD : (j + 1) * HD
                        ]
            return carry

        lax.fori_loop(0, 2, body, 0)
        far = (qy + 2) % NY
        for way, slot in ((RIGHT, 2 * mg), (LEFT, 2 * mg + 1)):
            send(
                ("kh", hh, mg, way),
                ps.at[hh, :, far, slot],
                kh.at[hh, mg, way],
                at_y(1 if way == RIGHT else 3, cc),
            )
        for slot in (2 * mg, 2 * mg + 1):
            send(("kv", hh, slot), ps.at[hh, oc, qy, slot], rk.at[hh, cc, 0, slot], sibling)
            local(("lk", hh, slot), ps.at[hh, cc, qy, slot], rk.at[hh, cc, 0, slot]).start()

    def near_keys(hh, mg, way):
        send_keys(hh, way, 2 * mg + 1 - way)

    def send_keys(hh, way, slot):
        step = 1 if way == RIGHT else 3
        for same in (1, 0):
            core = cc if same else oc
            send(
                ("ky", hh, way, slot, same),
                ps.at[hh, core, (qy + step) % NY, slot],
                rk.at[hh, cc, 1 + way, slot],
                at_y(step, core),
            )

    def relay_keys(hh, mg, way):
        slot = 2 * mg + way
        target = (qy + (1 if way == RIGHT else 3)) % NY
        receive(("kh", hh, mg, way), kh.at[hh, mg, way])
        for replica in (0, 1):
            ps[hh, replica, target, slot] = (
                ps[hh, replica, target, slot].astype(F32) + kh[hh, mg, way, replica].astype(F32)
            ).astype(BF)
        send_keys(hh, way, slot)

    def projected(hh, slot):
        loaded(("lk", hh, slot), rk.at[hh, cc, 0, slot])
        receive(("kv", hh, slot), rk.at[hh, oc, 0, slot])
        for way in (RIGHT, LEFT):
            for same in (1, 0):
                receive(
                    ("ky", hh, way, slot, same), rk.at[hh, cc if same else oc, 1 + way, slot]
                )

    root_scale = 1.0 / math.sqrt(HD)

    def attend(hh, slot):
        projected(hh, slot)
        loaded(("d", slot), do.at[slot])
        gain = k_gain[...]
        micro = (px + OFFSETS[slot]) % NX
        key_pre = rk[hh, 0, 0, slot].astype(F32)
        value = rk[hh, 1, 0, slot].astype(F32)
        for step in (1, 2):
            key_pre += rk[hh, 0, step, slot].astype(F32)
            value += rk[hh, 1, step, slot].astype(F32)
        value = value.astype(BF)
        inverse = lax.rsqrt(
            jnp.mean(key_pre * key_pre, axis=-1, keepdims=True) + EPSILON
        )
        key = (key_pre * inverse * gain).astype(BF)
        slots = lax.broadcasted_iota(jnp.int32, (ROWS, 2 * ROWS), 0)
        texts = lax.broadcasted_iota(jnp.int32, (ROWS, 2 * ROWS), 1) % ROWS
        first = tiles[0, 0, micro] * TILE_TOK
        second = first + tiles[0, 1, micro] * TILE_TOK
        seen = ((slots < first) & (texts >= starts[0, 0, micro])) | (
            (slots >= first) & (slots < second) & (texts >= starts[0, 1, micro])
        )
        visible = jnp.where(seen, 1.0, 0.0).astype(F32)
        value_grad = jnp.zeros((ROWS, HD), F32)
        normed_grad = jnp.zeros((ROWS, HD), F32)
        for g in range(0, GROUPS, 2):
            low = (hh * GROUPS + g) * HD
            query = jnp.concatenate(
                [qb[slot, :, low : low + HD], qb[slot, :, low + HD : low + 2 * HD]], axis=0
            )
            grad = jnp.concatenate(
                [do[slot, :, low : low + HD], do[slot, :, low + HD : low + 2 * HD]], axis=0
            )
            scores = (
                lax.dot_general(key, query, NT, preferred_element_type=F32) * root_scale
            )
            weights = jnp.exp(scores) * visible
            total = jnp.sum(weights, axis=0, keepdims=True)
            probability = weights * (1.0 / jnp.where(total > 0, total, 1.0))
            prob_grad = lax.dot_general(value, grad, NT, preferred_element_type=F32)
            delta = jnp.sum(probability * prob_grad, axis=0, keepdims=True)
            score_grad = (probability * (prob_grad - delta)).astype(BF)
            value_grad += jnp.dot(
                probability.astype(BF), grad, preferred_element_type=F32
            )
            normed_grad += jnp.dot(score_grad, query, preferred_element_type=F32)
        scaled = normed_grad * root_scale * gain
        key_grad = inverse * scaled - key_pre * (inverse * inverse * inverse) * jnp.mean(
            scaled * key_pre, axis=-1, keepdims=True
        )
        gs[hh, 0, slot] = key_grad.astype(BF)
        gs[hh, 1, slot] = value_grad.astype(BF)
        for way in (slot % 2, 1 - slot % 2):
            for same in (1, 0):
                kind = cc if same else oc
                send(
                    ("g", hh, slot, way, same),
                    gs.at[hh, kind, slot],
                    ga.at[hh, qy, slot, cc],
                    at_y(1 if way == RIGHT else 3, kind),
                )
        send(("g", hh, slot), gs.at[hh, oc, slot], ga.at[hh, qy, slot, cc], sibling)
        local(("lg", hh, slot), gs.at[hh, cc, slot], ga.at[hh, qy, slot, cc]).start()

    def near_grads(hh, slot, way):
        source = (qy + (3 if way == RIGHT else 1)) % NY
        for same in (1, 0):
            receive(("g", hh, slot, way, same), ga.at[hh, source, slot, cc if same else oc])
        return source

    def relay_grads(hh, slot):
        way = slot % 2
        block = ga.at[hh, near_grads(hh, slot, way), slot]
        send(("gh", hh, slot), block, block, at_y(1 if way == RIGHT else 3, cc))

    def gathered(hh, slot):
        loaded(("lg", hh, slot), ga.at[hh, qy, slot, cc])
        receive(("g", hh, slot), ga.at[hh, qy, slot, oc])
        for way in (RIGHT, LEFT):
            near_grads(hh, slot, way)
        receive(("gh", hh, slot), ga.at[hh, (qy + 2) % NY, slot])

    def weight_term(hh, distance):
        for slot in range(NX):
            gathered(hh, slot)
        block = (zz + distance) % NZ
        lhs = ft[pl.ds(pl.multiple_of(block * 256, 256), 256), :]

        def body(n, carry):
            columns = pl.ds(pl.multiple_of(n * 256, 256), 256)
            grads = jnp.concatenate(
                [ga[hh, n * 2 + j].reshape(8 * ROWS, HD) for j in (0, 1)], axis=1
            )
            pw[hh, distance, :, columns] = jnp.dot(lhs, grads, preferred_element_type=F32)
            return carry

        lax.fori_loop(0, 2, body, 0)

    def weight_pair(hh, distance):
        for slot in range(NX):
            gathered(hh, slot)
        ends = (distance, NZ - distance)

        def body(n, carry):
            columns = pl.ds(pl.multiple_of(n * 256, 256), 256)
            grads = jnp.concatenate(
                [ga[hh, n * 2 + j].reshape(8 * ROWS, HD) for j in (0, 1)], axis=1
            )
            rows = [
                ft[pl.ds(pl.multiple_of((zz + end) % NZ * 256, 256), 256), :] for end in ends
            ]
            total = jnp.dot(
                jnp.concatenate(rows, axis=0), grads, preferred_element_type=F32
            )
            pw[hh, ends[0], :, columns] = total[:256]
            pw[hh, ends[1], :, columns] = total[256:]
            return carry

        lax.fori_loop(0, 2, body, 0)

    def scatter(hh, n):
        k, second = (n + 1) // 2, n % 2
        if n == 1:
            sent(("rs", hh, 0))
        in_flight["rs", hh, n] = copies = []
        for direction in (RIGHT, LEFT):
            piece = 1 - direction if second else direction
            distance = HALF - k if direction == RIGHT else HALF + k
            total = pw[hh, distance, piece * ROWS : (piece + 1) * ROWS, :]
            if n > 1:
                arrived = rb.at[hh, direction, k - 1, piece]
                receive(("rs", direction, hh, k - 1, piece), arrived)
                total = total + arrived[...].astype(F32)
            sb[hh, direction, k, piece] = total.astype(BF)
            copies.append(
                send(
                    ("rs", direction, hh, k, piece),
                    sb.at[hh, direction, k, piece],
                    rb.at[hh, direction, k, piece],
                    onward(direction),
                )
            )

    factor = 1.0 / (NX * NZ * 2)

    def scatter_done(hh):
        for direction in (RIGHT, LEFT):
            for piece in (0, 1):
                receive(
                    ("rs", direction, hh, HALF - 1, piece), rb.at[hh, direction, HALF - 1, piece]
                )

        def finished(piece):
            total = (
                pw[hh, 0, pl.ds(pl.multiple_of(piece * ROWS, ROWS), ROWS), :]
                + rb[hh, RIGHT, HALF - 1, piece].astype(F32)
                + rb[hh, LEFT, HALF - 1, piece].astype(F32)
            )
            return (total * factor).astype(BF)

        other = finished(oc)
        for j in range(NY):
            osd[hh, j] = other[:, j * HD : (j + 1) * HD]
        send(("ow", hh), osd.at[hh], ow.at[cc, hh], sibling)
        own = finished(cc)
        for j in range(NY):
            ow[cc, hh, j] = own[:, j * HD : (j + 1) * HD]

    def feature_term(hh, pair, part):
        for slot in (2 * pair, 2 * pair + 1):
            gathered(hh, slot)

        def body(n, carry):
            columns = pl.ds(pl.multiple_of(n * 256, 256), 256)
            grads = jnp.concatenate(
                [ga[hh, j, 2 * pair : 2 * pair + 2].reshape(4 * ROWS, HD) for j in range(NY)],
                axis=1,
            )
            weights = wb[hh, n].reshape(256, NY * HD)
            total = lax.dot_general(grads, weights, NT, preferred_element_type=F32)
            for i in (0, 1):
                slot = 2 * pair + i
                terms = [total[(2 * i + r) * ROWS : (2 * i + r + 1) * ROWS] for r in (0, 1)]
                if hh == 0:
                    for r in (0, 1):
                        af[slot, r, :, columns] = terms[r]
                else:
                    terms = [terms[r] + af[slot, r, :, columns] for r in (0, 1)]
                    af[slot, 0, :, columns] = jnp.where(cc == 0, terms[0], terms[1])
                    ds[slot, :, columns] = jnp.where(cc == 0, terms[1], terms[0]).astype(BF)
            return carry

        lax.fori_loop(part * HALF, part * HALF + HALF, body, 0)
        if hh == 1 and part == 1:
            for slot in (2 * pair + 1, 2 * pair):
                send(("df", slot), ds.at[slot], dr.at[slot], sibling)

    half = ROWS // 2

    def feature_far():
        receive(("df", 3), dr.at[3])
        dx[3] = (af[3, 0] + dr[3].astype(F32)).astype(BF)
        for way in (RIGHT, LEFT):
            send(
                ("xh", way),
                dx.at[3, pl.ds(way * half, half)],
                xh.at[way],
                at_x(1 if way == RIGHT else 3),
            )

    def feature_send(way, second):
        slot = 1 if way == RIGHT else 2
        receive(("df", slot), dr.at[slot])
        low = half * (way if second else 1 - way)
        total = af[slot, 0, low : low + half] + dr[slot, low : low + half].astype(F32)
        if second:
            receive(("xh", way), xh.at[way])
            total = total + xh[way].astype(F32)
        dx[slot, low : low + half] = total.astype(BF)
        rows = pl.ds(low, half)
        send(
            ("xr", way, second),
            dx.at[slot, rows],
            xr.at[way, rows],
            at_x(1 if way == RIGHT else 3),
        )

    def feature_done():
        receive(("df", 0), dr.at[0])
        for way in (RIGHT, LEFT):
            for second in (0, 1):
                low = half * (way if second else 1 - way)
                receive(("xr", way, second), xr.at[way, pl.ds(low, half)])
        total = af[0, 0] + dr[0].astype(F32)
        for way in (RIGHT, LEFT):
            total = total + xr[way].astype(F32)
        dx[0] = total.astype(BF)
        local("of", dx.at[0], out_f.at[0]).start()

    norm_queries(2)
    gather(0, 0)
    norm_queries(3)
    transpose_features(0, 0)
    transpose_features(0, 1)
    gather(0, 1)
    norm_queries(0)
    gather(0, 2)
    norm_queries(1)
    gather(0, 3)
    relay_features(1)
    relay_features(0)
    transpose_features(2, 1)
    gather(0, 4)
    transpose_features(1, 1)
    gather(0, 5)
    transpose_features(2, 0)
    transpose_features(1, 0)
    gather(0, 6)
    transpose_features(3, 1)
    gather(1, 0)
    far_features()
    transpose_features(3, 0)
    gather(1, 1)
    project(0, 0)
    near_keys(0, 0, 0)
    near_keys(0, 0, 1)
    gather(1, 2)
    project(0, 1)
    near_keys(0, 1, 0)
    gather(1, 3)
    near_keys(0, 1, 1)
    relay_keys(0, 0, 1)
    relay_keys(0, 0, 0)
    gather(1, 4)
    relay_keys(0, 1, 0)
    relay_keys(0, 1, 1)
    gather(1, 5)
    attend(0, 0)
    attend(0, 2)
    gather(1, 6)
    attend(0, 1)
    relay_grads(0, 0)
    attend(0, 3)
    relay_grads(0, 2)
    relay_grads(0, 1)
    project(1, 1)
    relay_grads(0, 3)
    project(1, 0)
    feature_term(0, 0, 0)
    near_keys(1, 0, 0)
    relay_keys(1, 1, 0)
    relay_keys(1, 1, 1)
    near_keys(1, 1, 1)
    near_keys(1, 1, 0)
    weight_term(0, 4)
    scatter(0, 0)
    relay_keys(1, 0, 1)
    weight_pair(0, 3)
    feature_term(0, 0, 1)
    near_keys(1, 0, 1)
    relay_keys(1, 0, 0)
    scatter(0, 1)
    attend(1, 2)
    scatter(0, 2)
    attend(1, 3)
    weight_pair(0, 2)
    weight_term(0, 0)
    scatter(0, 3)
    relay_grads(1, 2)
    attend(1, 1)
    relay_grads(1, 3)
    scatter(0, 4)
    attend(1, 0)
    weight_pair(0, 1)
    relay_grads(1, 1)
    scatter(0, 5)
    feature_term(0, 1, 0)
    relay_grads(1, 0)
    feature_term(0, 1, 1)
    scatter(0, 6)
    feature_term(1, 1, 0)
    weight_term(1, 4)
    scatter(1, 0)
    feature_term(1, 1, 1)
    weight_term(1, 0)
    weight_pair(1, 3)
    scatter(1, 1)
    feature_term(1, 0, 0)
    feature_far()
    scatter(1, 2)
    feature_term(1, 0, 1)
    feature_send(1, 0)
    weight_pair(1, 2)
    scatter(1, 3)
    scatter_done(0)
    weight_pair(1, 1)
    feature_send(0, 0)
    scatter(1, 4)
    feature_send(0, 1)
    scatter(1, 5)
    feature_send(1, 1)
    scatter(1, 6)
    scatter_done(1)
    feature_done()

    for hh in (0, 1):
        receive(("ow", hh), ow.at[oc, hh])
    for kind, out in ((0, out_k), (1, out_v)):
        for hh in (0, 1):
            for j in range(NY):
                local(
                    ("out", kind, hh, j),
                    ow.at[kind, hh, j],
                    out.at[0, :, pl.ds((2 * j + hh) * HD, HD)],
                ).start()
    for kind, out in ((0, out_k), (1, out_v)):
        for hh in (0, 1):
            for j in range(NY):
                local(
                    ("out", kind, hh, j),
                    ow.at[kind, hh, j],
                    out.at[0, :, pl.ds((2 * j + hh) * HD, HD)],
                ).wait()
    local("of", dx.at[0], out_f.at[0]).wait()
    for copy in started:
        copy.wait_send()
    assert len(ids) <= N_SEMS and len(local_ids) <= 64, (len(ids), len(local_ids))


def copy_results(a, b, c, x, y, z, hold_a, hold_b, hold_c, sems):
    parts = ((a, hold_a, x), (b, hold_b, y), (c, hold_c, z))
    reads = [pltpu.make_async_copy(p[0], p[1], sems.at[n]) for n, p in enumerate(parts)]
    writes = [pltpu.make_async_copy(p[1], p[2], sems.at[3 + n]) for n, p in enumerate(parts)]
    for copy in reads:
        copy.start()
    for n in range(3):
        reads[n].wait()
        writes[n].start()
    for copy in writes:
        copy.wait()


def per_device(
    queries, grad_out, features, w_key, w_value, q_gain, k_gain, tile_counts, image_starts
):
    hbm = pl.BlockSpec(memory_space=pl.ANY)
    vmem = pl.BlockSpec(memory_space=pltpu.VMEM)
    smem = pl.BlockSpec(memory_space=pltpu.SMEM)
    tiles = jnp.transpose(tile_counts, (1, 2, 0))
    starts = jnp.transpose(image_starts, (1, 2, 0))
    flops = 3 * 2 * 512 * WIDTH * 2048 + 8 * 8 * 4 * 2 * ROWS * ROWS * HD
    results = pl.pallas_call(
        kernel,
        out_shape=(
            jax.ShapeDtypeStruct((1, ROWS, WIDTH), BF),
            jax.ShapeDtypeStruct((1, ROWS, 1024), BF),
            jax.ShapeDtypeStruct((1, ROWS, 1024), BF),
        ),
        in_specs=[hbm, hbm, hbm, hbm, hbm, vmem, vmem, smem, smem],
        out_specs=(hbm, hbm, hbm),
        scratch_shapes=[
            pltpu.VMEM((4, ROWS, WIDTH), BF),
            pltpu.VMEM((4, ROWS, WIDTH), BF),
            pltpu.VMEM((4, 2, ROWS, WIDTH), BF),
            pltpu.VMEM((WIDTH, 8 * ROWS), BF),
            pltpu.VMEM((2, NZ, 2, ROWS, NY * HD), BF),
            pltpu.VMEM((2, 2, NY, 4, ROWS, HD), BF),
            pltpu.VMEM((2, 2, 3, 4, ROWS, HD), BF),
            pltpu.VMEM((2, 2, 2, 2, ROWS, HD), BF),
            pltpu.VMEM((2, 2, 4, ROWS, HD), BF),
            pltpu.VMEM((2, NY, 4, 2, ROWS, HD), BF),
            pltpu.VMEM((2, NZ, 2 * ROWS, NY * HD), F32),
            pltpu.VMEM((2, 2, HALF, 2, ROWS, NY * HD), BF),
            pltpu.VMEM((2, 2, HALF, 2, ROWS, NY * HD), BF),
            pltpu.VMEM((2, NY, ROWS, HD), BF),
            pltpu.VMEM((2, 2, NY, ROWS, HD), BF),
            pltpu.VMEM((4, ROWS, WIDTH), BF),
            pltpu.VMEM((4, ROWS, WIDTH), BF),
            pltpu.VMEM((4, 2, ROWS, WIDTH), F32),
            pltpu.VMEM((4, ROWS, WIDTH), BF),
            pltpu.VMEM((2, 64, WIDTH), BF),
            pltpu.VMEM((2, ROWS, WIDTH), BF),
            pltpu.SemaphoreType.DMA((N_SEMS,)),
            pltpu.SemaphoreType.DMA((N_SEMS,)),
            pltpu.SemaphoreType.DMA((64,)),
        ],
        compiler_params=pltpu.CompilerParams(
            collective_id=0, has_side_effects=True, vmem_limit_bytes=58 << 20
        ),
        cost_estimate=pl.CostEstimate(
            flops=flops, bytes_accessed=8 << 20, transcendentals=1 << 20
        ),
        name="cross_attention_backward",
    )(queries, grad_out, features, w_key, w_value, q_gain, k_gain, tiles, starts)
    return pl.pallas_call(
        copy_results,
        out_shape=tuple(jax.ShapeDtypeStruct(r.shape, r.dtype) for r in results),
        in_specs=[hbm, hbm, hbm],
        out_specs=(hbm, hbm, hbm),
        scratch_shapes=[pltpu.VMEM(r.shape, r.dtype) for r in results]
        + [pltpu.SemaphoreType.DMA((6,))],
        name="copy_results",
    )(*results)


def solution(mesh):
    in_specs = (
        P("pipe", None, "dp", "mp"),
        P("pipe", None, "dp", "mp"),
        P("pipe", "dp", "mp"),
        P("pipe", ("mp", "dp"), None),
        P("pipe", ("mp", "dp"), None),
        P("pipe", None),
        P("pipe", None),
        P(None, "dp", None),
        P(None, "dp", None),
    )
    out_specs = (
        P("pipe", "dp", "mp"),
        P("pipe", ("mp", "dp"), None),
        P("pipe", ("mp", "dp"), None),
    )
    return jax.shard_map(
        per_device, mesh=mesh, in_specs=in_specs, out_specs=out_specs, check_vma=False
    )
```

```python
import math

import jax
import jax.numpy as jnp
from jax import lax
from jax.experimental import pallas as pl
from jax.experimental.pallas import tpu as pltpu
from jax.sharding import PartitionSpec as P

TILE_TOK = 16
EPSILON = 1e-05
NX, NY, NZ = 4, 4, 8
HD = 128
ROWS = 128
WIDTH = 2048
GROUPS = 8
OFFSETS = (0, 1, 3, 2)
RIGHT, LEFT = 0, 1
HALF = NZ // 2
BF = jnp.bfloat16
F32 = jnp.float32
MESH = pl.DeviceIdType.MESH
N_SEMS = 224
NT = (((1,), (1,)), ((), ()))


def kernel(
    queries,
    grad_out,
    features,
    w_key,
    w_value,
    q_gain,
    k_gain,
    tiles,
    starts,
    out_f,
    out_k,
    out_v,
    qb,
    do,
    fa,
    ft,
    wb,
    ps,
    rk,
    kh,
    gs,
    ga,
    pw,
    sb,
    rb,
    osd,
    ow,
    ds,
    dr,
    af,
    dx,
    xh,
    xr,
    send_sems,
    recv_sems,
    local_sems,
):
    px = lax.axis_index("pipe")
    dd = lax.axis_index("dp")
    qy = lax.axis_index("mp")
    zz = dd // 2
    cc = dd % 2
    oc = 1 - cc
    kinds = (w_key, w_value)

    def at_x(step):
        return ((px + step) % NX, dd, qy)

    def at_y(step, core):
        return (px, zz * 2 + core, (qy + step) % NY)

    def at_z(step):
        return (px, ((zz + step) % NZ) * 2 + cc, qy)

    sibling = (px, zz * 2 + oc, qy)

    ids = {}
    started = []

    def sem_of(key):
        return ids.setdefault(key, len(ids))

    def remote(key, src, dst, device):
        n = sem_of(key)
        return pltpu.make_async_remote_copy(
            src_ref=src,
            dst_ref=dst,
            send_sem=send_sems.at[n],
            recv_sem=recv_sems.at[n],
            device_id=device,
            device_id_type=MESH,
        )

    def send(key, src, dst, device):
        copy = remote(key, src, dst, device)
        copy.start()
        started.append(copy)
        return copy

    waited = set()

    def receive(key, dst):
        if key not in waited:
            waited.add(key)
            remote(key, dst, dst, sibling).wait_recv()

    local_ids = {}

    def local(key, src, dst):
        n = local_ids.setdefault(key, len(local_ids))
        return pltpu.make_async_copy(src, dst, local_sems.at[n])

    def loaded(key, dst):
        if key not in waited:
            waited.add(key)
            local(key, dst, dst).wait()

    barrier = pltpu.get_barrier_semaphore()
    partners = [sibling, at_z(1), at_z(NZ - 1)]
    partners += [at_x(step) for step in (1, 3)]
    partners += [at_y(step, core) for step in (1, 3) for core in (cc, oc)]
    for device in partners:
        pl.semaphore_signal(barrier, inc=1, device_id=device, device_id_type=MESH)

    def weight_columns(ref, hh, j):
        return ref.at[0, :, pl.ds((2 * j + hh) * HD, HD)]

    for kind in (0, 1):

        @pl.when(cc == kind)
        def _():
            for hh in (0, 1):
                for j in range(NY):
                    local(
                        ("lw", hh, j),
                        weight_columns(kinds[kind], hh, j),
                        wb.at[hh, zz, cc, :, pl.ds(j * HD, HD)],
                    ).start()

    local("f", features.at[0], fa.at[0, cc]).start()
    for slot in range(NX):
        local(("q", slot), queries.at[0, (px + OFFSETS[slot]) % NX], qb.at[slot]).start()
        local(("d", slot), grad_out.at[0, (px + OFFSETS[slot]) % NX], do.at[slot]).start()

    pl.semaphore_wait(barrier, len(partners))

    for kind in (0, 1):

        @pl.when(oc == kind)
        def _():
            for hh in (0, 1):
                for j in range(NY):
                    remote(
                        ("w", hh, j),
                        weight_columns(kinds[kind], hh, j),
                        wb.at[hh, zz, cc, :, pl.ds(j * HD, HD)],
                        sibling,
                    ).start()

    for hh in (0, 1):
        for j in range(NY):
            piece = wb.at[hh, zz, cc, :, pl.ds(j * HD, HD)]
            started.append(remote(("w", hh, j), piece, piece, sibling))

    send(("fx", 3), features.at[0], fa.at[2, cc], at_x(1))
    send(("fx", 1), features.at[0], fa.at[1, cc], at_x(3))
    send(("fs", 0), features.at[0], fa.at[0, cc], sibling)

    def origin(direction, k):
        return (zz - k + NZ) % NZ if direction == RIGHT else (zz + k) % NZ

    def onward(direction):
        return at_z(1 if direction == RIGHT else NZ - 1)

    in_flight = {}

    def sent(key):
        for copy in in_flight.pop(key):
            copy.wait_send()
            started[:] = [other for other in started if other is not copy]

    def gather(hh, n):
        k, second = n // 2, n % 2
        if n == 0:
            own_weights(hh)
        before = {(0, 1): (0, 0), (1, 0): (0, 5), (1, 1): (0, 6)}.get((hh, n))
        if before:
            sent(("ag", *before))
        in_flight["ag", hh, n] = copies = []
        for direction in (RIGHT, LEFT):
            piece = 1 - direction if second else direction
            block = wb.at[hh, origin(direction, k), piece]
            if k:
                receive(("ag", direction, hh, k - 1, piece), block)
            copies.append(
                send(("ag", direction, hh, k, piece), block, block, onward(direction))
            )

    def gather_done(hh):
        for k, second in ((HALF - 2, 1), (HALF - 1, 0)):
            for direction in (RIGHT, LEFT):
                piece = 1 - direction if second else direction
                receive(
                    ("ag", direction, hh, k, piece),
                    wb.at[hh, origin(direction, k + 1), piece],
                )

    def own_weights(hh):
        for j in range(NY):
            piece = wb.at[hh, zz, cc, :, pl.ds(j * HD, HD)]
            loaded(("lw", hh, j), piece)
        for j in range(NY):
            piece = wb.at[hh, zz, oc, :, pl.ds(j * HD, HD)]
            receive(("w", hh, j), piece)

    def norm_queries(slot):
        loaded(("q", slot), qb.at[slot])
        gain = q_gain[...]

        def body(i, carry):
            for u in range(4):
                columns = pl.ds(pl.multiple_of((i * 4 + u) * HD, HD), HD)
                values = qb[slot, :, columns].astype(F32)
                inverse = lax.rsqrt(
                    jnp.mean(values * values, axis=-1, keepdims=True) + EPSILON
                )
                qb[slot, :, columns] = (values * inverse * gain).astype(BF)
            return carry

        lax.fori_loop(0, WIDTH // HD // 4, body, 0)

    def features_ready(slot, same):
        block = fa.at[slot, cc if same else oc]
        if not same:
            receive(("fs", slot), block)
        elif slot == 0:
            loaded("f", block)
        elif slot == 3:
            for way in (0, 1):
                receive(("fh", way), fa.at[3, cc, pl.ds(way * 64, 64)])
        else:
            receive(("fx", 1 if slot == 1 else 3), block)

    def relay_features(way):
        slot, rows = 1 + way, pl.ds(way * 64, 64)
        features_ready(slot, 1)
        send(("fh", way), fa.at[slot, cc, rows], fa.at[3, cc, rows], at_x(3 if way == 0 else 1))
        send(("fs", slot), fa.at[slot, cc], fa.at[slot, cc], sibling)

    def far_features():
        features_ready(3, 1)
        send(("fs", 3), fa.at[3, cc], fa.at[3, cc], sibling)

    def transpose_features(slot, same):
        features_ready(slot, same)
        replica = cc if same else oc
        place = pl.multiple_of((slot * 2 + replica) * ROWS, ROWS)

        def body(i, carry):
            for u in range(2):
                columns = pl.ds(pl.multiple_of((i * 2 + u) * HD, HD), HD)
                ft[columns, pl.ds(place, ROWS)] = fa[slot, replica, :, columns].T
            return carry

        lax.fori_loop(0, WIDTH // HD // 2, body, 0)

    def project(hh, mg):
        gather_done(hh)
        for slot in (2 * mg, 2 * mg + 1):
            for same in (1, 0):
                features_ready(slot, same)

        def body(n, carry):
            rows = fa[2 * mg : 2 * mg + 2].reshape(4 * ROWS, WIDTH)
            columns = pl.ds(pl.multiple_of(n * 256, 256), 256)
            weights = wb[hh, :, :, :, columns].reshape(WIDTH, 256)
            total = jnp.dot(rows, weights, preferred_element_type=F32).astype(BF)
            for slot in (0, 1):
                for replica in (0, 1):
                    low = (slot * 2 + replica) * ROWS
                    for j in (0, 1):
                        ps[hh, replica, n * 2 + j, 2 * mg + slot] = total[
                            low : low + ROWS, j * HD : (j + 1) * HD
                        ]
            return carry

        lax.fori_loop(0, 2, body, 0)
        far = (qy + 2) % NY
        for way, slot in ((RIGHT, 2 * mg), (LEFT, 2 * mg + 1)):
            send(
                ("kh", hh, mg, way),
                ps.at[hh, :, far, slot],
                kh.at[hh, mg, way],
                at_y(1 if way == RIGHT else 3, cc),
            )
        for slot in (2 * mg, 2 * mg + 1):
            send(("kv", hh, slot), ps.at[hh, oc, qy, slot], rk.at[hh, cc, 0, slot], sibling)
            local(("lk", hh, slot), ps.at[hh, cc, qy, slot], rk.at[hh, cc, 0, slot]).start()

    def near_keys(hh, mg, way):
        send_keys(hh, way, 2 * mg + 1 - way)

    def send_keys(hh, way, slot):
        step = 1 if way == RIGHT else 3
        for same in (1, 0):
            core = cc if same else oc
            send(
                ("ky", hh, way, slot, same),
                ps.at[hh, core, (qy + step) % NY, slot],
                rk.at[hh, cc, 1 + way, slot],
                at_y(step, core),
            )

    def relay_keys(hh, mg, way):
        slot = 2 * mg + way
        target = (qy + (1 if way == RIGHT else 3)) % NY
        receive(("kh", hh, mg, way), kh.at[hh, mg, way])
        for replica in (0, 1):
            ps[hh, replica, target, slot] = (
                ps[hh, replica, target, slot].astype(F32) + kh[hh, mg, way, replica].astype(F32)
            ).astype(BF)
        send_keys(hh, way, slot)

    def projected(hh, slot):
        loaded(("lk", hh, slot), rk.at[hh, cc, 0, slot])
        receive(("kv", hh, slot), rk.at[hh, oc, 0, slot])
        for way in (RIGHT, LEFT):
            for same in (1, 0):
                receive(
                    ("ky", hh, way, slot, same), rk.at[hh, cc if same else oc, 1 + way, slot]
                )

    root_scale = 1.0 / math.sqrt(HD)

    def attend(hh, slot):
        projected(hh, slot)
        loaded(("d", slot), do.at[slot])
        gain = k_gain[...]
        micro = (px + OFFSETS[slot]) % NX
        key_pre = rk[hh, 0, 0, slot].astype(F32)
        value = rk[hh, 1, 0, slot].astype(F32)
        for step in (1, 2):
            key_pre += rk[hh, 0, step, slot].astype(F32)
            value += rk[hh, 1, step, slot].astype(F32)
        value = value.astype(BF)
        inverse = lax.rsqrt(
            jnp.mean(key_pre * key_pre, axis=-1, keepdims=True) + EPSILON
        )
        key = (key_pre * inverse * gain).astype(BF)
        slots = lax.broadcasted_iota(jnp.int32, (ROWS, 2 * ROWS), 0)
        texts = lax.broadcasted_iota(jnp.int32, (ROWS, 2 * ROWS), 1) % ROWS
        first = tiles[0, 0, micro] * TILE_TOK
        second = first + tiles[0, 1, micro] * TILE_TOK
        seen = ((slots < first) & (texts >= starts[0, 0, micro])) | (
            (slots >= first) & (slots < second) & (texts >= starts[0, 1, micro])
        )
        visible = jnp.where(seen, 1.0, 0.0).astype(F32)
        value_grad = jnp.zeros((ROWS, HD), F32)
        normed_grad = jnp.zeros((ROWS, HD), F32)
        for g in range(0, GROUPS, 2):
            low = (hh * GROUPS + g) * HD
            query = jnp.concatenate(
                [qb[slot, :, low : low + HD], qb[slot, :, low + HD : low + 2 * HD]], axis=0
            )
            grad = jnp.concatenate(
                [do[slot, :, low : low + HD], do[slot, :, low + HD : low + 2 * HD]], axis=0
            )
            scores = (
                lax.dot_general(key, query, NT, preferred_element_type=F32) * root_scale
            )
            weights = jnp.exp(scores) * visible
            total = jnp.sum(weights, axis=0, keepdims=True)
            probability = weights * (1.0 / jnp.where(total > 0, total, 1.0))
            prob_grad = lax.dot_general(value, grad, NT, preferred_element_type=F32)
            delta = jnp.sum(probability * prob_grad, axis=0, keepdims=True)
            score_grad = (probability * (prob_grad - delta)).astype(BF)
            value_grad += jnp.dot(
                probability.astype(BF), grad, preferred_element_type=F32
            )
            normed_grad += jnp.dot(score_grad, query, preferred_element_type=F32)
        scaled = normed_grad * root_scale * gain
        key_grad = inverse * scaled - key_pre * (inverse * inverse * inverse) * jnp.mean(
            scaled * key_pre, axis=-1, keepdims=True
        )
        gs[hh, 0, slot] = key_grad.astype(BF)
        gs[hh, 1, slot] = value_grad.astype(BF)
        for way in (slot % 2, 1 - slot % 2):
            for same in (1, 0):
                kind = cc if same else oc
                send(
                    ("g", hh, slot, way, same),
                    gs.at[hh, kind, slot],
                    ga.at[hh, qy, slot, cc],
                    at_y(1 if way == RIGHT else 3, kind),
                )
        send(("g", hh, slot), gs.at[hh, oc, slot], ga.at[hh, qy, slot, cc], sibling)
        local(("lg", hh, slot), gs.at[hh, cc, slot], ga.at[hh, qy, slot, cc]).start()

    def near_grads(hh, slot, way):
        source = (qy + (3 if way == RIGHT else 1)) % NY
        for same in (1, 0):
            receive(("g", hh, slot, way, same), ga.at[hh, source, slot, cc if same else oc])
        return source

    def relay_grads(hh, slot):
        way = slot % 2
        block = ga.at[hh, near_grads(hh, slot, way), slot]
        send(("gh", hh, slot), block, block, at_y(1 if way == RIGHT else 3, cc))

    def gathered(hh, slot):
        loaded(("lg", hh, slot), ga.at[hh, qy, slot, cc])
        receive(("g", hh, slot), ga.at[hh, qy, slot, oc])
        for way in (RIGHT, LEFT):
            near_grads(hh, slot, way)
        receive(("gh", hh, slot), ga.at[hh, (qy + 2) % NY, slot])

    def weight_term(hh, distance):
        for slot in range(NX):
            gathered(hh, slot)
        block = (zz + distance) % NZ
        lhs = ft[pl.ds(pl.multiple_of(block * 256, 256), 256), :]

        def body(n, carry):
            columns = pl.ds(pl.multiple_of(n * 256, 256), 256)
            grads = jnp.concatenate(
                [ga[hh, n * 2 + j].reshape(8 * ROWS, HD) for j in (0, 1)], axis=1
            )
            pw[hh, distance, :, columns] = jnp.dot(lhs, grads, preferred_element_type=F32)
            return carry

        lax.fori_loop(0, 2, body, 0)

    def weight_pair(hh, distance):
        for slot in range(NX):
            gathered(hh, slot)
        ends = (distance, NZ - distance)

        def body(n, carry):
            columns = pl.ds(pl.multiple_of(n * 256, 256), 256)
            grads = jnp.concatenate(
                [ga[hh, n * 2 + j].reshape(8 * ROWS, HD) for j in (0, 1)], axis=1
            )
            rows = [
                ft[pl.ds(pl.multiple_of((zz + end) % NZ * 256, 256), 256), :] for end in ends
            ]
            total = jnp.dot(
                jnp.concatenate(rows, axis=0), grads, preferred_element_type=F32
            )
            pw[hh, ends[0], :, columns] = total[:256]
            pw[hh, ends[1], :, columns] = total[256:]
            return carry

        lax.fori_loop(0, 2, body, 0)

    def scatter(hh, n):
        k, second = (n + 1) // 2, n % 2
        if n == 1:
            sent(("rs", hh, 0))
        in_flight["rs", hh, n] = copies = []
        for direction in (RIGHT, LEFT):
            piece = 1 - direction if second else direction
            distance = HALF - k if direction == RIGHT else HALF + k
            total = pw[hh, distance, piece * ROWS : (piece + 1) * ROWS, :]
            if n > 1:
                arrived = rb.at[hh, direction, k - 1, piece]
                receive(("rs", direction, hh, k - 1, piece), arrived)
                total = total + arrived[...].astype(F32)
            sb[hh, direction, k, piece] = total.astype(BF)
            copies.append(
                send(
                    ("rs", direction, hh, k, piece),
                    sb.at[hh, direction, k, piece],
                    rb.at[hh, direction, k, piece],
                    onward(direction),
                )
            )

    factor = 1.0 / (NX * NZ * 2)

    def scatter_done(hh):
        for direction in (RIGHT, LEFT):
            for piece in (0, 1):
                receive(
                    ("rs", direction, hh, HALF - 1, piece), rb.at[hh, direction, HALF - 1, piece]
                )

        def finished(piece):
            total = (
                pw[hh, 0, pl.ds(pl.multiple_of(piece * ROWS, ROWS), ROWS), :]
                + rb[hh, RIGHT, HALF - 1, piece].astype(F32)
                + rb[hh, LEFT, HALF - 1, piece].astype(F32)
            )
            return (total * factor).astype(BF)

        other = finished(oc)
        for j in range(NY):
            osd[hh, j] = other[:, j * HD : (j + 1) * HD]
        send(("ow", hh), osd.at[hh], ow.at[cc, hh], sibling)
        own = finished(cc)
        for j in range(NY):
            ow[cc, hh, j] = own[:, j * HD : (j + 1) * HD]

    def feature_term(hh, pair, part):
        for slot in (2 * pair, 2 * pair + 1):
            gathered(hh, slot)

        def body(n, carry):
            columns = pl.ds(pl.multiple_of(n * 256, 256), 256)
            grads = jnp.concatenate(
                [ga[hh, j, 2 * pair : 2 * pair + 2].reshape(4 * ROWS, HD) for j in range(NY)],
                axis=1,
            )
            weights = wb[hh, n].reshape(256, NY * HD)
            total = lax.dot_general(grads, weights, NT, preferred_element_type=F32)
            for i in (0, 1):
                slot = 2 * pair + i
                terms = [total[(2 * i + r) * ROWS : (2 * i + r + 1) * ROWS] for r in (0, 1)]
                if hh == 0:
                    for r in (0, 1):
                        af[slot, r, :, columns] = terms[r]
                else:
                    terms = [terms[r] + af[slot, r, :, columns] for r in (0, 1)]
                    af[slot, 0, :, columns] = jnp.where(cc == 0, terms[0], terms[1])
                    ds[slot, :, columns] = jnp.where(cc == 0, terms[1], terms[0]).astype(BF)
            return carry

        lax.fori_loop(part * HALF, part * HALF + HALF, body, 0)
        if hh == 1 and part == 1:
            for slot in (2 * pair + 1, 2 * pair):
                send(("df", slot), ds.at[slot], dr.at[slot], sibling)

    half = ROWS // 2

    def feature_far():
        receive(("df", 3), dr.at[3])
        dx[3] = (af[3, 0] + dr[3].astype(F32)).astype(BF)
        for way in (RIGHT, LEFT):
            send(
                ("xh", way),
                dx.at[3, pl.ds(way * half, half)],
                xh.at[way],
                at_x(1 if way == RIGHT else 3),
            )

    def feature_send(way, second):
        slot = 1 if way == RIGHT else 2
        receive(("df", slot), dr.at[slot])
        low = half * (way if second else 1 - way)
        total = af[slot, 0, low : low + half] + dr[slot, low : low + half].astype(F32)
        if second:
            receive(("xh", way), xh.at[way])
            total = total + xh[way].astype(F32)
        dx[slot, low : low + half] = total.astype(BF)
        rows = pl.ds(low, half)
        send(
            ("xr", way, second),
            dx.at[slot, rows],
            xr.at[way, rows],
            at_x(1 if way == RIGHT else 3),
        )

    def feature_done():
        receive(("df", 0), dr.at[0])
        for way in (RIGHT, LEFT):
            for second in (0, 1):
                low = half * (way if second else 1 - way)
                receive(("xr", way, second), xr.at[way, pl.ds(low, half)])
        total = af[0, 0] + dr[0].astype(F32)
        for way in (RIGHT, LEFT):
            total = total + xr[way].astype(F32)
        dx[0] = total.astype(BF)
        local("of", dx.at[0], out_f.at[0]).start()

    norm_queries(2)
    gather(0, 0)
    norm_queries(3)
    transpose_features(0, 0)
    transpose_features(0, 1)
    gather(0, 1)
    norm_queries(0)
    gather(0, 2)
    norm_queries(1)
    gather(0, 3)
    relay_features(1)
    relay_features(0)
    transpose_features(2, 1)
    gather(0, 4)
    transpose_features(1, 1)
    gather(0, 5)
    transpose_features(2, 0)
    transpose_features(1, 0)
    gather(0, 6)
    transpose_features(3, 1)
    gather(1, 0)
    far_features()
    transpose_features(3, 0)
    gather(1, 1)
    project(0, 0)
    near_keys(0, 0, 0)
    near_keys(0, 0, 1)
    gather(1, 2)
    project(0, 1)
    near_keys(0, 1, 0)
    gather(1, 3)
    near_keys(0, 1, 1)
    relay_keys(0, 0, 1)
    relay_keys(0, 0, 0)
    gather(1, 4)
    relay_keys(0, 1, 0)
    relay_keys(0, 1, 1)
    gather(1, 5)
    attend(0, 0)
    attend(0, 2)
    gather(1, 6)
    attend(0, 1)
    relay_grads(0, 0)
    attend(0, 3)
    relay_grads(0, 2)
    relay_grads(0, 1)
    project(1, 1)
    relay_grads(0, 3)
    project(1, 0)
    feature_term(0, 0, 0)
    near_keys(1, 0, 0)
    relay_keys(1, 1, 0)
    relay_keys(1, 1, 1)
    near_keys(1, 1, 1)
    near_keys(1, 1, 0)
    weight_term(0, 4)
    scatter(0, 0)
    relay_keys(1, 0, 1)
    weight_pair(0, 3)
    feature_term(0, 0, 1)
    near_keys(1, 0, 1)
    relay_keys(1, 0, 0)
    scatter(0, 1)
    attend(1, 2)
    scatter(0, 2)
    attend(1, 3)
    weight_pair(0, 2)
    weight_term(0, 0)
    scatter(0, 3)
    relay_grads(1, 2)
    attend(1, 1)
    relay_grads(1, 3)
    scatter(0, 4)
    attend(1, 0)
    weight_pair(0, 1)
    relay_grads(1, 1)
    scatter(0, 5)
    feature_term(0, 1, 0)
    relay_grads(1, 0)
    feature_term(0, 1, 1)
    scatter(0, 6)
    feature_term(1, 1, 0)
    weight_term(1, 4)
    scatter(1, 0)
    feature_term(1, 1, 1)
    weight_term(1, 0)
    weight_pair(1, 3)
    scatter(1, 1)
    feature_term(1, 0, 0)
    feature_far()
    scatter(1, 2)
    feature_term(1, 0, 1)
    feature_send(1, 0)
    weight_pair(1, 2)
    scatter(1, 3)
    scatter_done(0)
    weight_pair(1, 1)
    feature_send(0, 0)
    scatter(1, 4)
    feature_send(0, 1)
    scatter(1, 5)
    feature_send(1, 1)
    scatter(1, 6)
    scatter_done(1)
    feature_done()

    for hh in (0, 1):
        receive(("ow", hh), ow.at[oc, hh])
    for kind, out in ((0, out_k), (1, out_v)):
        for hh in (0, 1):
            for j in range(NY):
                local(
                    ("out", kind, hh, j),
                    ow.at[kind, hh, j],
                    out.at[0, :, pl.ds((2 * j + hh) * HD, HD)],
                ).start()
    for kind, out in ((0, out_k), (1, out_v)):
        for hh in (0, 1):
            for j in range(NY):
                local(
                    ("out", kind, hh, j),
                    ow.at[kind, hh, j],
                    out.at[0, :, pl.ds((2 * j + hh) * HD, HD)],
                ).wait()
    local("of", dx.at[0], out_f.at[0]).wait()
    for copy in started:
        copy.wait_send()
    assert len(ids) <= N_SEMS and len(local_ids) <= 64, (len(ids), len(local_ids))


def copy_results(a, b, c, x, y, z, sems):
    parts = ((a, x), (b, y), (c, z))
    copies = [pltpu.make_async_copy(p[0], p[1], sems.at[n]) for n, p in enumerate(parts)]
    for copy in copies:
        copy.start()
    for copy in copies:
        copy.wait()


def per_device(
    queries, grad_out, features, w_key, w_value, q_gain, k_gain, tile_counts, image_starts
):
    hbm = pl.BlockSpec(memory_space=pl.ANY)
    vmem = pl.BlockSpec(memory_space=pltpu.VMEM)
    smem = pl.BlockSpec(memory_space=pltpu.SMEM)
    tiles = jnp.transpose(tile_counts, (1, 2, 0))
    starts = jnp.transpose(image_starts, (1, 2, 0))
    flops = 3 * 2 * 512 * WIDTH * 2048 + 8 * 8 * 4 * 2 * ROWS * ROWS * HD
    results = pl.pallas_call(
        kernel,
        out_shape=(
            pltpu.VMEM((1, ROWS, WIDTH), BF),
            pltpu.VMEM((1, ROWS, 1024), BF),
            pltpu.VMEM((1, ROWS, 1024), BF),
        ),
        in_specs=[hbm, hbm, hbm, hbm, hbm, vmem, vmem, smem, smem],
        out_specs=(vmem, vmem, vmem),
        scratch_shapes=[
            pltpu.VMEM((4, ROWS, WIDTH), BF),
            pltpu.VMEM((4, ROWS, WIDTH), BF),
            pltpu.VMEM((4, 2, ROWS, WIDTH), BF),
            pltpu.VMEM((WIDTH, 8 * ROWS), BF),
            pltpu.VMEM((2, NZ, 2, ROWS, NY * HD), BF),
            pltpu.VMEM((2, 2, NY, 4, ROWS, HD), BF),
            pltpu.VMEM((2, 2, 3, 4, ROWS, HD), BF),
            pltpu.VMEM((2, 2, 2, 2, ROWS, HD), BF),
            pltpu.VMEM((2, 2, 4, ROWS, HD), BF),
            pltpu.VMEM((2, NY, 4, 2, ROWS, HD), BF),
            pltpu.VMEM((2, NZ, 2 * ROWS, NY * HD), F32),
            pltpu.VMEM((2, 2, HALF, 2, ROWS, NY * HD), BF),
            pltpu.VMEM((2, 2, HALF, 2, ROWS, NY * HD), BF),
            pltpu.VMEM((2, NY, ROWS, HD), BF),
            pltpu.VMEM((2, 2, NY, ROWS, HD), BF),
            pltpu.VMEM((4, ROWS, WIDTH), BF),
            pltpu.VMEM((4, ROWS, WIDTH), BF),
            pltpu.VMEM((4, 2, ROWS, WIDTH), F32),
            pltpu.VMEM((4, ROWS, WIDTH), BF),
            pltpu.VMEM((2, 64, WIDTH), BF),
            pltpu.VMEM((2, ROWS, WIDTH), BF),
            pltpu.SemaphoreType.DMA((N_SEMS,)),
            pltpu.SemaphoreType.DMA((N_SEMS,)),
            pltpu.SemaphoreType.DMA((64,)),
        ],
        compiler_params=pltpu.CompilerParams(
            collective_id=0, has_side_effects=True, vmem_limit_bytes=58 << 20
        ),
        cost_estimate=pl.CostEstimate(
            flops=flops, bytes_accessed=8 << 20, transcendentals=1 << 20
        ),
        name="cross_attention_backward",
    )(queries, grad_out, features, w_key, w_value, q_gain, k_gain, tiles, starts)
    held = [pltpu.with_memory_space_constraint(r, pltpu.VMEM) for r in results]
    return pl.pallas_call(
        copy_results,
        out_shape=tuple(jax.ShapeDtypeStruct(r.shape, r.dtype) for r in results),
        in_specs=[vmem, vmem, vmem],
        out_specs=(hbm, hbm, hbm),
        scratch_shapes=[pltpu.SemaphoreType.DMA((3,))],
        name="copy_results",
    )(*held)


def solution(mesh):
    in_specs = (
        P("pipe", None, "dp", "mp"),
        P("pipe", None, "dp", "mp"),
        P("pipe", "dp", "mp"),
        P("pipe", ("mp", "dp"), None),
        P("pipe", ("mp", "dp"), None),
        P("pipe", None),
        P("pipe", None),
        P(None, "dp", None),
        P(None, "dp", None),
    )
    out_specs = (
        P("pipe", "dp", "mp"),
        P("pipe", ("mp", "dp"), None),
        P("pipe", ("mp", "dp"), None),
    )
    return jax.shard_map(
        per_device, mesh=mesh, in_specs=in_specs, out_specs=out_specs, check_vma=False
    )
```
